128 devices in a mesh: layer: 4 (over x), node: 32 (over z, y, core).
Axes of the slice: x: 4, y: 4, z: 4, core: 2. Of those that a mesh axis runs over, the one named last changes fastest.
Arguments:
- features: bfloat16 [4, 16384, 512], P(None, 'node'), may hold values from -6 to 6
- weights: bfloat16 [4, 512, 512], P('layer'), may hold values from -0.25 to 0.25
- boundary: int32 [4, 32, 128], P(None, 'node'), may hold values from 0 to 511
- pick_index: int32 [4, 32, 32, 64], P(None, 'node'), may hold values from 0 to 127
- counts: int32 [4, 32, 4], P(None, 'node'), may hold values from 1 to 12, 20 in all within a row
- tile_cols: int32 [4, 32, 20], P(None, 'node'), may hold values from 0 to 23
- tile_vals: bfloat16 [4, 32, 20, 128, 128], P(None, 'node'), may hold values from -0.25 to 0.25
Outputs:
- jumping: bfloat16 [4, 16384, 2048], P(None, 'node', 'layer')
The draws below stay inside these ranges and needn't reach their ends.
Inputs may be any that keep to these rules, and one draw needn't show every extreme that they name: boundary[c, n, k] is a row index within device n's own 512 rows of span c. pick_index[c, p, q, b] names which of device p's offered rows is device q's b-th boundary row from p; every list has exactly 64 entries. For each span and device the counts sum to 20, and the largest is exactly 12. `tile_cols`: column tiles 0 .. 3 are the device's own rows, the next 4 its rows of the earlier span, the rest its boundary rows.
All inputs are finite; a program needn't handle non-finite values.
Results may differ from the reference program's by a relative error of at most 0.02.
Values may be sent and summed in bfloat16 or wider, within the bound.
No kernel may reach another device: no remote copies, remote signals or barrier semaphores. Data moves between devices by JAX's collectives and lax.ppermute only.
A program may use at most 128 MiB of HBM per device.

```python
import math
import jax
import jax.numpy as jnp
import numpy as np
from jax import lax

D = 512
ROWS = 512
SPANS = 4
TILE = 128
TILE_MOST = 12
BOUND = 64
BSET = 128
LAYERS = 4
NODES = 16384
ROW_TILES = 4
COL_TILES = 24
TILES_DEV = 20
N_NODE = 32


def plant(result, key, smallest, largest):
    place = [jax.random.randint(jax.random.fold_in(key, axis), (), 0, length) for axis, length in enumerate(result.shape)]
    longest = result.shape.index(max(result.shape))
    beside = place[:longest] + [(place[longest] + 1) % result.shape[longest]] + place[longest + 1:]
    return result.at[tuple(place)].set(smallest).at[tuple(beside)].set(largest)


def block_levels(key, extent, cuts, smallest, top_value):
    level, own = 1.0, jax.random.fold_in(key, 6)
    for axis_at, blocks in cuts:
        steps = jnp.exp(jax.random.uniform(jax.random.fold_in(own, axis_at), (blocks,), jnp.float32, smallest / len(cuts), top_value / len(cuts)))
        level = level * jnp.repeat(steps, extent[axis_at] // blocks).reshape([-1 if axis == axis_at else 1 for axis in range(len(extent))])
    return level


def length_profile(count, total, most, lean):
    weights = [(1 << 20) // math.isqrt(standing ** lean) + 1 for standing in range(2, count + 1)]
    surplus, given = total - most - (count - 1), [1] * (count - 1)
    while surplus > 0:
        candidates = [i for i in range(count - 1) if given[i] < most]
        whole, remaining = sum([weights[i] for i in candidates]), surplus
        for i in candidates:
            extra = min(most - given[i], max(1, remaining * weights[i] // whole), surplus)
            given[i] = given[i] + extra
            surplus = surplus - extra
    return np.array([most] + given)


def ragged(key, number_of, total, limit, lean):
    if number_of == 2:
        one = jax.random.randint(key, (), max(1, total - limit), min(limit, total - 1) + 1)
        return jnp.stack([one, total - one])
    tallies = jnp.asarray(length_profile(number_of, total, limit, lean), jnp.int32)
    twos = (number_of - 1) // 2
    donor, sink = tallies[1:1 + 2 * twos:2], tallies[2:2 + 2 * twos:2]
    margin = jnp.minimum(donor - 1, limit - sink)
    passed = jax.random.randint(jax.random.fold_in(key, 1), (twos,), 0, 1 << 20) % (margin + 1)
    tallies = tallies.at[1:1 + 2 * twos:2].set(donor - passed).at[2:2 + 2 * twos:2].set(sink + passed)
    return tallies[jax.random.permutation(jax.random.fold_in(key, 2), number_of)]


def gaussian(key, shape, spread, most, cuts=(), kind=jnp.bfloat16):
    factor_of = block_levels(key, shape, cuts, -0.22, 0.18) if cuts else 1.0
    array = jax.random.normal(key, shape, jnp.float32) * spread * factor_of
    return jnp.minimum(jnp.maximum(array, -most), most).astype(kind)


def setup_inputs(seed: int = 0) -> dict:
    splits = jax.random.split(jax.random.key(seed), 8)
    features = gaussian(splits[0], (SPANS, NODES, D), 1.0, 6.0, ((1, 32),))
    weights = gaussian(splits[1], (LAYERS, D, D), D ** -0.5, 0.25, ((0, 4),))
    boundary = plant(jax.random.randint(splits[2], (SPANS, N_NODE, BSET), 0, ROWS), jax.random.fold_in(splits[2], 1), 0, ROWS - 1).astype(jnp.int32)
    pick_index = plant(jax.random.randint(splits[3], (SPANS, N_NODE, N_NODE, BOUND), 0, BSET), jax.random.fold_in(splits[3], 1), 0, BSET - 1).astype(jnp.int32)
    counts = jax.vmap(lambda own: ragged(own, ROW_TILES, TILES_DEV, TILE_MOST, 2))(jax.random.split(splits[4], SPANS * N_NODE)).reshape((SPANS, N_NODE, ROW_TILES)).astype(jnp.int32)
    tile_cols = plant(jax.random.randint(splits[5], (SPANS, N_NODE, TILES_DEV), 0, COL_TILES), jax.random.fold_in(splits[5], 1), 0, COL_TILES - 1).astype(jnp.int32)
    tile_vals = gaussian(splits[6], (SPANS, N_NODE, TILES_DEV, TILE, TILE), (TILES_DEV * TILE // ROW_TILES) ** -0.5, 0.25, ((1, 32),))
    return {"features": features, "weights": weights, "boundary": boundary, "pick_index": pick_index, "counts": counts, "tile_cols": tile_cols, "tile_vals": tile_vals}


def span_layer(hidden, previous, weight, boundary, pick_index, counts, tile_cols, tile_vals):
    blocks = hidden.reshape(N_NODE, ROWS, D)
    prev_blocks = previous.reshape(N_NODE, ROWS, D)
    exported = jnp.take_along_axis(blocks, boundary[:, :, None], axis=1)
    senders = jnp.arange(N_NODE).astype(jnp.int32)

    def per_node(node_id):
        picked = lax.dynamic_index_in_dim(pick_index, node_id, 1, keepdims=False)
        fetched = exported[senders[:, None], picked]
        col_space = jnp.concatenate([blocks[node_id], prev_blocks[node_id], fetched.reshape(N_NODE * BOUND, D)], 0)
        col_tiles = col_space.reshape(COL_TILES, TILE, D)
        chosen = col_tiles[tile_cols[node_id]]
        products = jnp.einsum('fab,fbd->fad', tile_vals[node_id].astype(jnp.float32), chosen.astype(jnp.float32))
        tile_ends = jnp.cumsum(counts[node_id]).astype(jnp.int32)
        flat_ids = jnp.arange(TILES_DEV).astype(jnp.int32)
        owner_tile = jnp.sum((flat_ids[:, None] >= tile_ends[None, :]).astype(jnp.int32), axis=1)
        row_ids = jnp.arange(ROW_TILES).astype(jnp.int32)
        onehot = (owner_tile[None, :] == row_ids[:, None]).astype(jnp.float32)
        aggregate = jnp.einsum('rf,fad->rad', onehot, products).reshape(ROWS, D).astype(jnp.bfloat16)
        linear = jnp.dot(aggregate, weight, preferred_element_type=jnp.float32)
        return jnp.maximum(linear, 0.0).astype(jnp.bfloat16)

    return lax.map(per_node, senders).reshape(N_NODE * ROWS, D)


def reference(features, weights, boundary, pick_index, counts, tile_cols, tile_vals):
    stored = [jnp.zeros((NODES, D), jnp.bfloat16) for layer_id in range(LAYERS)]
    results = []
    for span_id in range(SPANS):
        hidden = features[span_id]
        layer_outs = []
        for layer_id in range(LAYERS):
            fresh = span_layer(hidden, stored[layer_id], weights[layer_id], boundary[span_id],
                               pick_index[span_id], counts[span_id], tile_cols[span_id], tile_vals[span_id])
            stored[layer_id] = hidden
            layer_outs.append(fresh)
            hidden = fresh
        results.append(jnp.concatenate(layer_outs, axis=1))
    return jnp.stack(results)
```

```python
import functools

import jax
import jax.numpy as jnp
from jax import lax
from jax.experimental import pallas as pl
from jax.experimental.pallas import tpu as pltpu
from jax.sharding import PartitionSpec as P

TILE = 128
ANY = pl.BlockSpec(memory_space=pl.ANY)
SMEM = pl.BlockSpec(memory_space=pltpu.SMEM)
VMEM = pl.BlockSpec(memory_space=pltpu.VMEM)


def offer(rows, export_sel, chooser, sent_ref):
    exported = jnp.dot(export_sel, rows, preferred_element_type=jnp.float32).astype(jnp.bfloat16)
    sent = jnp.dot(chooser, exported, preferred_element_type=jnp.float32)
    sent_ref[...] = sent.astype(jnp.bfloat16)


def first_kernel(span_ref, features_ref, export_ref, chooser_ref, sent_ref, rows, sem):
    copy = pltpu.make_async_copy(features_ref.at[span_ref[0]], rows, sem)
    copy.start()
    copy.wait()
    offer(rows[...], export_ref[...], chooser_ref[...], sent_ref)


def layer_kernel(
    layer_id, first, last,
    span_ref, counts_ref, cols_ref, current_ref, previous_ref, received_ref, vals_ref, weights_ref,
    export_ref, chooser_ref, *rest,
):
    if last:
        out_ref, space, tiles, weight, total, sems = rest
    else:
        out_ref, sent_ref, space, tiles, weight, total, sems = rest
    span = span_ref[0]
    row_count = total.shape[0]
    if first:
        current_src = current_ref.at[span]
        previous_src = previous_ref.at[jnp.maximum(span - 1, 0)]
    else:
        current_src, previous_src = current_ref, previous_ref
    own = space.at[pl.ds(0, row_count)]
    earlier = space.at[pl.ds(row_count, row_count)]
    others = space.at[pl.ds(2 * row_count, received_ref.shape[0])]
    copies = [
        pltpu.make_async_copy(vals_ref.at[span, 0], tiles, sems.at[0]),
        pltpu.make_async_copy(current_src, own, sems.at[1]),
        pltpu.make_async_copy(previous_src, earlier, sems.at[2]),
        pltpu.make_async_copy(received_ref, others, sems.at[3]),
        pltpu.make_async_copy(weights_ref.at[layer_id], weight, sems.at[4]),
    ]
    for copy in copies:
        copy.start()
    total[...] = jnp.zeros_like(total)
    for copy in copies:
        copy.wait()

    @pl.when(span == 0)
    def _():
        earlier[...] = jnp.zeros_like(earlier)

    ends = []
    reached = 0
    for r in range(counts_ref.shape[1] - 1):
        reached = reached + counts_ref[span, r]
        ends.append(reached)
    for f in range(cols_ref.shape[1]):
        owner = sum((f >= end).astype(jnp.int32) for end in ends)
        row_at = pl.ds(pl.multiple_of(owner * TILE, TILE), TILE)
        col_at = pl.ds(pl.multiple_of(cols_ref[span, f] * TILE, TILE), TILE)
        total[row_at, :] += jnp.dot(tiles[f], space[col_at, :], preferred_element_type=jnp.float32)
    aggregate = total[...].astype(jnp.bfloat16)
    linear = jnp.dot(aggregate, weight[...], preferred_element_type=jnp.float32)
    fresh = jnp.maximum(linear, 0.0).astype(jnp.bfloat16)
    out_ref[...] = fresh
    if not last:
        offer(fresh, export_ref[...], chooser_ref[...], sent_ref)


def on_device(features, weights, boundary, pick_index, counts, tile_cols, tile_vals):
    spans, row_count, width = features.shape
    layers = lax.axis_size("layer")
    nodes = lax.axis_size("node")
    picks, offered = pick_index.shape[3], boundary.shape[2]
    span = lax.axis_index("layer")
    span_arr = span.astype(jnp.int32)[None]
    all_weights = lax.all_gather(weights[0], "layer")
    listed = lax.dynamic_index_in_dim(boundary, span, 0, keepdims=False)[0]
    export_sel = (listed[:, None] == jnp.arange(row_count, dtype=jnp.int32)).astype(jnp.bfloat16)
    lists = lax.dynamic_index_in_dim(pick_index, span, 0, keepdims=False)[0].reshape(-1)
    chooser = (lists[:, None] == jnp.arange(offered, dtype=jnp.int32)).astype(jnp.bfloat16)
    counts, tile_cols = counts[:, 0], tile_cols[:, 0]
    sent_shape = jax.ShapeDtypeStruct((nodes * picks, width), jnp.bfloat16)
    out_shape = jax.ShapeDtypeStruct((row_count, width), jnp.bfloat16)
    params = pltpu.CompilerParams(vmem_limit_bytes=40 << 20)
    sent = pl.pallas_call(
        first_kernel,
        out_shape=sent_shape,
        in_specs=[SMEM, ANY, VMEM, VMEM],
        out_specs=VMEM,
        scratch_shapes=[pltpu.VMEM((row_count, width), jnp.bfloat16), pltpu.SemaphoreType.DMA],
        compiler_params=params,
    )(span_arr, features, export_sel, chooser)
    current = previous = features
    outputs = []
    ring = [(i, (i + 1) % layers) for i in range(layers)]
    for layer_id in range(layers):
        first, last = layer_id == 0, layer_id == layers - 1
        received = lax.all_to_all(
            sent.reshape(nodes, picks, width), "node", split_axis=0, concat_axis=0, tiled=True
        ).reshape(nodes * picks, width)
        results = pl.pallas_call(
            functools.partial(layer_kernel, layer_id, first, last),
            out_shape=[out_shape] if last else [out_shape, sent_shape],
            in_specs=[SMEM, SMEM, SMEM, ANY, ANY, ANY, ANY, ANY, VMEM, VMEM],
            out_specs=[VMEM] if last else [VMEM, VMEM],
            scratch_shapes=[
                pltpu.VMEM((2 * row_count + nodes * picks, width), jnp.bfloat16),
                pltpu.VMEM(tile_vals.shape[2:], jnp.bfloat16),
                pltpu.VMEM((width, width), jnp.bfloat16),
                pltpu.VMEM((row_count, width), jnp.float32),
                pltpu.SemaphoreType.DMA((5,)),
            ],
            compiler_params=params,
        )(span_arr, counts, tile_cols, current, previous, received, tile_vals, all_weights, export_sel, chooser)
        outputs.append(results[0])
        if not last:
            current, sent = results
            previous = lax.ppermute(current, "layer", ring)
    return lax.all_to_all(jnp.stack(outputs), "layer", split_axis=0, concat_axis=0, tiled=True)


def solution(mesh):
    return jax.shard_map(
        on_device,
        mesh=mesh,
        in_specs=(
            P(None, "node", None),
            P("layer", None, None),
            P(None, "node", None),
            P(None, "node", None, None),
            P(None, "node", None),
            P(None, "node", None),
            P(None, "node", None, None, None),
        ),
        out_specs=P(None, "node", "layer"),
        check_vma=False,
    )
```

```python
import functools

import jax
import jax.numpy as jnp
from jax import lax
from jax.experimental import pallas as pl
from jax.experimental.pallas import tpu as pltpu
from jax.sharding import PartitionSpec as P

TILE = 128
ANY = pl.BlockSpec(memory_space=pl.ANY)
SMEM = pl.BlockSpec(memory_space=pltpu.SMEM)
VMEM = pl.BlockSpec(memory_space=pltpu.VMEM)


def offer(rows, export_sel, chooser, sent_ref):
    exported = jnp.dot(export_sel, rows, preferred_element_type=jnp.float32).astype(jnp.bfloat16)
    sent = jnp.dot(chooser, exported, preferred_element_type=jnp.float32)
    sent_ref[...] = sent.astype(jnp.bfloat16)


def first_kernel(span_ref, features_ref, export_ref, chooser_ref, sent_ref, rows, sem):
    copy = pltpu.make_async_copy(features_ref.at[span_ref[0]], rows, sem)
    copy.start()
    copy.wait()
    offer(rows[...], export_ref[...], chooser_ref[...], sent_ref)


def layer_kernel(
    layer_id, first, last,
    span_ref, counts_ref, cols_ref, current_ref, previous_ref, received_ref, vals_ref, export_ref, chooser_ref, *rest,
):
    weight_refs, rest = rest[:4], rest[4:]
    if last:
        out_ref, space, tiles, weight, total, sems = rest
    else:
        out_ref, sent_ref, space, tiles, weight, total, sems = rest
    span = span_ref[0]
    row_count = total.shape[0]
    if first:
        current_src = current_ref.at[span]
        previous_src = previous_ref.at[jnp.maximum(span - 1, 0)]
    else:
        current_src, previous_src = current_ref, previous_ref
    own = space.at[pl.ds(0, row_count)]
    earlier = space.at[pl.ds(row_count, row_count)]
    others = space.at[pl.ds(2 * row_count, received_ref.shape[0])]
    for distance, source in enumerate(weight_refs):
        @pl.when((span + len(weight_refs) - distance) % len(weight_refs) == layer_id)
        def _():
            pltpu.make_async_copy(source, weight, sems.at[4]).start()

    copies = [
        pltpu.make_async_copy(vals_ref.at[span, 0], tiles, sems.at[0]),
        pltpu.make_async_copy(current_src, own, sems.at[1]),
        pltpu.make_async_copy(previous_src, earlier, sems.at[2]),
        pltpu.make_async_copy(received_ref, others, sems.at[3]),
    ]
    for copy in copies:
        copy.start()
    total[...] = jnp.zeros_like(total)
    for copy in copies:
        copy.wait()
    pltpu.make_async_copy(weight_refs[0], weight, sems.at[4]).wait()

    @pl.when(span == 0)
    def _():
        earlier[...] = jnp.zeros_like(earlier)

    ends = []
    reached = 0
    for r in range(counts_ref.shape[1] - 1):
        reached = reached + counts_ref[span, r]
        ends.append(reached)
    for f in range(cols_ref.shape[1]):
        owner = sum((f >= end).astype(jnp.int32) for end in ends)
        row_at = pl.ds(pl.multiple_of(owner * TILE, TILE), TILE)
        col_at = pl.ds(pl.multiple_of(cols_ref[span, f] * TILE, TILE), TILE)
        total[row_at, :] += jnp.dot(tiles[f], space[col_at, :], preferred_element_type=jnp.float32)
    aggregate = total[...].astype(jnp.bfloat16)
    linear = jnp.dot(aggregate, weight[...], preferred_element_type=jnp.float32)
    fresh = jnp.maximum(linear, 0.0).astype(jnp.bfloat16)
    out_ref[...] = fresh
    if not last:
        offer(fresh, export_ref[...], chooser_ref[...], sent_ref)


def place_kernel(span_ref, *refs):
    spans = refs[-2].shape[0]
    out_ref, sems = refs[-2], refs[-1]
    layers = (len(refs) - 2) // spans
    span = span_ref[0]
    for layer_id in range(layers):
        @pl.when(span == layer_id)
        def _():
            copies = []
            for distance in range(spans):
                source = refs[layer_id * spans + distance]
                target = out_ref.at[(layer_id - distance) % spans]
                copies.append(pltpu.make_async_copy(source, target, sems.at[distance]))
            for copy in copies:
                copy.start()
            for copy in copies:
                copy.wait()


def shifted(block, distance, only=None):
    planes = lax.axis_size("layer")
    route = [(i, (i + distance) % planes) for i in range(planes)]
    if only is not None:
        route = [pair for pair in route if pair[1] == only]
    return lax.ppermute(block, "layer", route)


def on_device(features, weights, boundary, pick_index, counts, tile_cols, tile_vals):
    spans, row_count, width = features.shape
    layers = lax.axis_size("layer")
    nodes = lax.axis_size("node")
    picks, offered = pick_index.shape[3], boundary.shape[2]
    span = lax.axis_index("layer")
    span_arr = span.astype(jnp.int32)[None]
    listed = lax.dynamic_index_in_dim(boundary, span, 0, keepdims=False)[0]
    export_sel = (listed[:, None] == jnp.arange(row_count, dtype=jnp.int32)).astype(jnp.bfloat16)
    lists = lax.dynamic_index_in_dim(pick_index, span, 0, keepdims=False)[0].reshape(-1)
    chooser = (lists[:, None] == jnp.arange(offered, dtype=jnp.int32)).astype(jnp.bfloat16)
    counts, tile_cols = counts[:, 0], tile_cols[:, 0]
    sent_shape = jax.ShapeDtypeStruct((nodes * picks, width), jnp.bfloat16)
    out_shape = jax.ShapeDtypeStruct((row_count, width), jnp.bfloat16)
    params = pltpu.CompilerParams(vmem_limit_bytes=56 << 20)
    sent = pl.pallas_call(
        first_kernel,
        out_shape=sent_shape,
        in_specs=[SMEM, ANY, VMEM, VMEM],
        out_specs=VMEM,
        scratch_shapes=[pltpu.VMEM((row_count, width), jnp.bfloat16), pltpu.SemaphoreType.DMA],
        compiler_params=params,
    )(span_arr, features, export_sel, chooser)
    current = previous = features
    mine = weights[0]
    known = None
    placed = []
    for layer_id in range(layers):
        first, last = layer_id == 0, layer_id == layers - 1
        received = lax.all_to_all(
            sent.reshape(nodes, picks, width), "node", split_axis=0, concat_axis=0, tiled=True
        ).reshape(nodes * picks, width)
        if first:
            known = [mine] + [shifted(mine, distance) for distance in range(1, layers)]
        results = pl.pallas_call(
            functools.partial(layer_kernel, layer_id, first, last),
            out_shape=[out_shape] if last else [out_shape, sent_shape],
            in_specs=[SMEM, SMEM, SMEM, ANY, ANY, ANY, ANY, VMEM, VMEM] + [ANY] * layers,
            out_specs=[VMEM] if last else [VMEM, VMEM],
            scratch_shapes=[
                pltpu.VMEM((2 * row_count + nodes * picks, width), jnp.bfloat16),
                pltpu.VMEM(tile_vals.shape[2:], jnp.bfloat16),
                pltpu.VMEM((width, width), jnp.bfloat16),
                pltpu.VMEM((row_count, width), jnp.float32),
                pltpu.SemaphoreType.DMA((5,)),
            ],
            compiler_params=params,
        )(span_arr, counts, tile_cols, current, previous, received, tile_vals, export_sel, chooser, *known)
        current = results[0]
        if not last:
            sent = results[1]
        previous = shifted(current, 1, layer_id if last else None)
        placed += [current, previous, shifted(current, 2, layer_id), shifted(current, 3, layer_id)]
    return pl.pallas_call(
        place_kernel,
        out_shape=jax.ShapeDtypeStruct(features.shape, features.dtype),
        in_specs=[SMEM] + [ANY] * len(placed),
        out_specs=ANY,
        scratch_shapes=[pltpu.SemaphoreType.DMA((spans,))],
        compiler_params=params,
    )(span_arr, *placed)


def solution(mesh):
    return jax.shard_map(
        on_device,
        mesh=mesh,
        in_specs=(
            P(None, "node", None),
            P("layer", None, None),
            P(None, "node", None),
            P(None, "node", None, None),
            P(None, "node", None),
            P(None, "node", None),
            P(None, "node", None, None, None),
        ),
        out_specs=P(None, "node", "layer"),
        check_vma=False,
    )
```

```python
import functools

import jax
import jax.numpy as jnp
from jax import lax
from jax.experimental import pallas as pl
from jax.experimental.pallas import tpu as pltpu
from jax.sharding import PartitionSpec as P

TILE = 128
SIDE = 4
CORES = 2
EXTRA = 16
ANY = pl.BlockSpec(memory_space=pl.ANY)
SMEM = pl.BlockSpec(memory_space=pltpu.SMEM)
VMEM = pl.BlockSpec(memory_space=pltpu.VMEM)
PLACES = [(z, y, core) for z in range(SIDE) for y in range(SIDE) for core in range(CORES)]


def node_of(z, y, core):
    return ((z % SIDE) * SIDE + y % SIDE) * CORES + core


def along(block, distance, phase):
    route = []
    for z, y, core in PLACES:
        if core == phase:
            target = node_of(z, y + distance, core)
        else:
            target = node_of(z + distance, y, core)
        route.append((node_of(z, y, core), target))
    return lax.ppermute(block, "node", route)


def other_core(block):
    route = [(node_of(z, y, core), node_of(z, y, 1 - core)) for z, y, core in PLACES]
    return lax.ppermute(block, "node", route)


def to_plane(block, pairs):
    return lax.ppermute(block, "layer", pairs)


def offered_rows(listed, rows):
    row_ids = lax.broadcasted_iota(jnp.int32, (rows.shape[0], listed.shape[1]), 0)
    selector = (row_ids == listed).astype(jnp.bfloat16)
    picked = lax.dot_general(
        selector, rows, (((0,), (0,)), ((), ())), preferred_element_type=jnp.float32
    )
    return picked.astype(jnp.bfloat16)


def first_kernel(place_ref, features_ref, boundary_ref, lists_ref, block_ref, rows, sem):
    span, node = place_ref[0], place_ref[1]
    copy = pltpu.make_async_copy(features_ref.at[span], rows, sem)
    copy.start()
    offered = boundary_ref.shape[2]
    nodes, picks = lists_ref.shape[2:]
    block_ref[pl.ds(offered, EXTRA), :] = jnp.zeros((EXTRA, block_ref.shape[1]), jnp.bfloat16)
    lists = lists_ref[span, 0].astype(jnp.float32).astype(jnp.bfloat16)
    for core in range(CORES):
        @pl.when(node % CORES == core)
        def _():
            for part in range(nodes // EXTRA):
                lanes = pl.ds(part * CORES * picks + core * picks, picks)
                block_ref[pl.ds(offered, EXTRA), lanes] = lists[part * EXTRA:(part + 1) * EXTRA]
    copy.wait()
    block_ref[pl.ds(0, offered), :] = offered_rows(boundary_ref[span], rows[...])


def layer_kernel(
    layer_id, first, last,
    place_ref, counts_ref, cols_ref, boundary_ref, current_ref, previous_ref, tiles_ref, *rest,
):
    weight_refs, rest = rest[:SIDE], rest[SIDE:]
    mine_refs, rest = rest[:SIDE], rest[SIDE:]
    theirs_refs, rest = rest[:SIDE], rest[SIDE:]
    outs = 1 if last else 3 if first else 2
    out_ref = rest[0]
    block_ref = None if last else rest[1]
    space, tiles, weight, total, sems = rest[outs:outs + 5]
    if first:
        wide_ref = rest[2]
        raw_lists, lists = rest[outs + 5:]
    span, node = place_ref[0], place_ref[1]
    row_count = total.shape[0]
    offered = boundary_ref.shape[2]
    z, y, core = node // (SIDE * CORES), (node // CORES) % SIDE, node % CORES
    copies = []

    def fetch(source, target):
        copy = pltpu.make_async_copy(source, target, sems.at[len(copies)])
        copies.append(copy)
        copy.start()

    each = mine_refs[0].shape[0] // SIDE
    for refs, kind in ((mine_refs, core), (theirs_refs, 1 - core)):
        for j in range(SIDE):
            for k in range(SIDE):
                dz = jnp.where(kind == 0, j, k)
                dy = jnp.where(kind == 0, k, j)
                chip = ((z + SIDE - dz) % SIDE) * SIDE + (y + SIDE - dy) % SIDE
                start = pl.multiple_of(2 * row_count + (chip * CORES + kind) * offered, offered)
                fetch(refs[j].at[pl.ds(k * each, offered)], space.at[pl.ds(start, offered)])
                if first:
                    source = refs[j].at[pl.ds(k * each + offered, EXTRA)]
                    fetch(source, raw_lists.at[chip * CORES + kind])
    if first:
        fetch(current_ref.at[span], space.at[pl.ds(0, row_count)])
        fetch(previous_ref.at[jnp.maximum(span - 1, 0)], space.at[pl.ds(row_count, row_count)])
        fetch(tiles_ref.at[span, 0], tiles)
    else:
        fetch(current_ref, space.at[pl.ds(0, row_count)])
        fetch(previous_ref, space.at[pl.ds(row_count, row_count)])
        fetch(tiles_ref, tiles)
    weight_sem = sems.at[len(copies)]
    for distance, source in enumerate(weight_refs):
        @pl.when((span + SIDE - distance) % SIDE == layer_id)
        def _():
            pltpu.make_async_copy(source, weight, weight_sem).start()
    total[...] = jnp.zeros_like(total)
    for copy in copies:
        copy.wait()
    pltpu.make_async_copy(weight_refs[0], weight, weight_sem).wait()

    @pl.when(span == 0)
    def _():
        space[pl.ds(row_count, row_count), :] = jnp.zeros((row_count, space.shape[1]), space.dtype)

    if first:
        lane_block = pl.ds(pl.multiple_of((node // EXTRA) * TILE, TILE), TILE)
        wanted = lax.broadcasted_iota(jnp.int32, (EXTRA, TILE), 0) == node % EXTRA
        lanes = lax.broadcasted_iota(jnp.int32, (1, TILE), 1)
        half = jnp.where(lanes >= TILE // CORES, offered, 0)
        for chip in range(SIDE * SIDE):
            both = raw_lists[chip * CORES, :, lane_block] + raw_lists[chip * CORES + 1, :, lane_block]
            row = jnp.sum(jnp.where(wanted, both.astype(jnp.float32), 0.0), axis=0, keepdims=True)
            lists[pl.ds(chip, 1), :] = row.astype(jnp.int32) + half
        slot_rows = lax.broadcasted_iota(jnp.int32, (CORES * offered, TILE), 0)

    ends = []
    reached = 0
    for r in range(counts_ref.shape[1] - 1):
        reached = reached + counts_ref[span, r]
        ends.append(reached)
    own_tiles = 2 * row_count // TILE
    for f in range(cols_ref.shape[1]):
        owner = sum((f >= end).astype(jnp.int32) for end in ends)
        col = cols_ref[span, f]
        if first:
            plain = lanes + TILE * (col % CORES)
            listed = lists[pl.ds(jnp.maximum(col - own_tiles, 0), 1), :]
            target = jnp.where(col < own_tiles, plain, listed)
            selector = (slot_rows == target).astype(jnp.bfloat16)
            wide = lax.dot_general(
                tiles[f], selector, (((1,), (1,)), ((), ())), preferred_element_type=jnp.float32
            ).astype(jnp.bfloat16)
            wide_ref[f] = wide
        else:
            wide = tiles[f]
        slot = jnp.where(col < own_tiles, col // CORES, col - own_tiles // CORES)
        row_at = pl.ds(pl.multiple_of(owner * TILE, TILE), TILE)
        slot_at = pl.ds(pl.multiple_of(slot * CORES * offered, CORES * offered), CORES * offered)
        total[row_at, :] += jnp.dot(wide, space[slot_at, :], preferred_element_type=jnp.float32)
    aggregate = total[...].astype(jnp.bfloat16)
    linear = jnp.dot(aggregate, weight[...], preferred_element_type=jnp.float32)
    fresh = jnp.maximum(linear, 0.0).astype(jnp.bfloat16)
    out_ref[...] = fresh
    if not last:
        block_ref[...] = offered_rows(boundary_ref[span], fresh)


def place_kernel(place_ref, *refs):
    out_ref, held, in_sems, out_sems = refs[-4:]
    spans = out_ref.shape[0]
    span = place_ref[0]
    parts = []
    for distance in range(spans):
        pieces = 2 if distance == 2 else 1
        rows = held.shape[1] // pieces
        parts += [(distance, rows * i, rows) for i in range(pieces)]
    for layer_id in range(spans):
        @pl.when(span == layer_id)
        def _():
            ins, outs = [], []
            for i, (distance, start, rows) in enumerate(parts):
                staged = held.at[distance, pl.ds(start, rows)]
                target = out_ref.at[(layer_id - distance) % spans, pl.ds(start, rows)]
                source = refs[layer_id * len(parts) + i]
                ins.append(pltpu.make_async_copy(source, staged, in_sems.at[i]))
                outs.append(pltpu.make_async_copy(staged, target, out_sems.at[i]))
            for copy in ins:
                copy.start()
            for i in range(len(parts)):
                ins[i].wait()
                outs[i].start()
            for copy in outs:
                copy.wait()


def on_device(features, weights, boundary, pick_index, counts, tile_cols, tile_vals):
    spans, row_count, width = features.shape
    layers = lax.axis_size("layer")
    nodes = lax.axis_size("node")
    picks, offered = pick_index.shape[3], boundary.shape[2]
    tile_total = tile_vals.shape[2]
    place = jnp.stack([lax.axis_index("layer"), lax.axis_index("node")]).astype(jnp.int32)
    counts, tile_cols = counts[:, 0], tile_cols[:, 0]
    rows_shape = jax.ShapeDtypeStruct((row_count, width), jnp.bfloat16)
    wide_shape = jax.ShapeDtypeStruct((tile_total, TILE, CORES * offered), jnp.bfloat16)
    block_shape = jax.ShapeDtypeStruct((offered, width), jnp.bfloat16)
    params = pltpu.CompilerParams(vmem_limit_bytes=56 << 20)
    block = pl.pallas_call(
        first_kernel,
        out_shape=jax.ShapeDtypeStruct((offered + EXTRA, width), jnp.bfloat16),
        in_specs=[SMEM, ANY, VMEM, VMEM],
        out_specs=VMEM,
        scratch_shapes=[pltpu.VMEM((row_count, width), jnp.bfloat16), pltpu.SemaphoreType.DMA],
        compiler_params=params,
    )(place, features, boundary, pick_index)
    current = previous = features
    tiles = tile_vals
    known = None
    placed = []
    for layer_id in range(layers):
        first, last = layer_id == 0, layer_id == layers - 1
        row = jnp.concatenate([block] + [along(block, k, 0) for k in range(1, SIDE)], 0)
        mine = [row] + [along(row, j, 1) for j in range(1, SIDE)]
        theirs = [other_core(part) for part in mine]
        if first:
            known = [weights[0]]
            for distance in range(1, layers):
                known.append(to_plane(weights[0], [(i, (i + distance) % layers) for i in range(layers)]))
        scratch = [
            pltpu.VMEM((2 * row_count + nodes * offered, width), jnp.bfloat16),
            pltpu.VMEM(tile_vals.shape[2:] if first else wide_shape.shape, jnp.bfloat16),
            pltpu.VMEM((width, width), jnp.bfloat16),
            pltpu.VMEM((row_count, width), jnp.float32),
            pltpu.SemaphoreType.DMA((2 * nodes + 4,)),
        ]
        if first:
            scratch += [
                pltpu.VMEM((nodes, EXTRA, width), jnp.bfloat16),
                pltpu.VMEM((SIDE * SIDE, TILE), jnp.int32),
            ]
        outs = [rows_shape] if last else [rows_shape, block_shape]
        if first:
            outs.append(wide_shape)
        results = pl.pallas_call(
            functools.partial(layer_kernel, layer_id, first, last),
            out_shape=outs,
            in_specs=[SMEM, SMEM, SMEM, VMEM] + [ANY] * (3 + 3 * SIDE),
            out_specs=[VMEM] * len(outs),
            scratch_shapes=scratch,
            compiler_params=params,
        )(place, counts, tile_cols, boundary, current, previous, tiles, *known, *mine, *theirs)
        current = results[0]
        if not last:
            block = results[1]
        if first:
            tiles = results[2]
        before, after, across = [(layer_id + step) % layers for step in (3, 1, 2)]
        half = row_count // 2
        if last:
            previous = to_plane(current, [(before, layer_id)])
        else:
            previous = to_plane(current, [(i, (i + 1) % layers) for i in range(layers)])
        relayed = to_plane(current[:half], [(across, before)])
        placed += [
            current,
            previous,
            to_plane(relayed, [(before, layer_id)]),
            to_plane(current[half:], [(across, layer_id)]),
            to_plane(current, [(after, layer_id)]),
        ]
    return pl.pallas_call(
        place_kernel,
        out_shape=jax.ShapeDtypeStruct(features.shape, features.dtype),
        in_specs=[SMEM] + [ANY] * len(placed),
        out_specs=ANY,
        scratch_shapes=[
            pltpu.VMEM(features.shape, features.dtype),
            pltpu.SemaphoreType.DMA((5,)),
            pltpu.SemaphoreType.DMA((5,)),
        ],
        compiler_params=params,
    )(place, *placed)


def solution(mesh):
    return jax.shard_map(
        on_device,
        mesh=mesh,
        in_specs=(
            P(None, "node", None),
            P("layer", None, None),
            P(None, "node", None),
            P(None, "node", None, None),
            P(None, "node", None),
            P(None, "node", None),
            P(None, "node", None, None, None),
        ),
        out_specs=P(None, "node", "layer"),
        check_vma=False,
    )
```

```python
import functools

import jax
import jax.numpy as jnp
from jax import lax
from jax.experimental import pallas as pl
from jax.experimental.pallas import tpu as pltpu
from jax.sharding import PartitionSpec as P

TILE = 128
SIDE = 4
CORES = 2
EXTRA = 16
ANY = pl.BlockSpec(memory_space=pl.ANY)
SMEM = pl.BlockSpec(memory_space=pltpu.SMEM)
VMEM = pl.BlockSpec(memory_space=pltpu.VMEM)
PLACES = [(z, y, core) for z in range(SIDE) for y in range(SIDE) for core in range(CORES)]


def node_of(z, y, core):
    return ((z % SIDE) * SIDE + y % SIDE) * CORES + core


def along(block, distance, phase):
    route = []
    for z, y, core in PLACES:
        if core == phase:
            target = node_of(z, y + distance, core)
        else:
            target = node_of(z + distance, y, core)
        route.append((node_of(z, y, core), target))
    return lax.ppermute(block, "node", route)


def other_core(block):
    route = [(node_of(z, y, core), node_of(z, y, 1 - core)) for z, y, core in PLACES]
    return lax.ppermute(block, "node", route)


def to_plane(block, pairs):
    return lax.ppermute(block, "layer", pairs)


def offered_rows(listed, rows):
    row_ids = lax.broadcasted_iota(jnp.int32, (rows.shape[0], listed.shape[1]), 0)
    selector = (row_ids == listed).astype(jnp.bfloat16)
    picked = lax.dot_general(
        selector, rows, (((0,), (0,)), ((), ())), preferred_element_type=jnp.float32
    )
    return picked.astype(jnp.bfloat16)


def first_kernel(place_ref, rows_ref, listed_ref, lists_ref, block_ref):
    node = place_ref[1]
    offered = listed_ref.shape[1]
    nodes, picks = lists_ref.shape
    block_ref[pl.ds(offered, EXTRA), :] = jnp.zeros((EXTRA, block_ref.shape[1]), jnp.bfloat16)
    lists = lists_ref[...].astype(jnp.float32).astype(jnp.bfloat16)
    for core in range(CORES):
        @pl.when(node % CORES == core)
        def _():
            for part in range(nodes // EXTRA):
                lanes = pl.ds(part * CORES * picks + core * picks, picks)
                block_ref[pl.ds(offered, EXTRA), lanes] = lists[part * EXTRA:(part + 1) * EXTRA]
    block_ref[pl.ds(0, offered), :] = offered_rows(listed_ref[...], rows_ref[...])


def layer_kernel(
    layer_id, first, last,
    place_ref, counts_ref, cols_ref, listed_ref, current_ref, previous_ref, tiles_ref, halves_ref, others_ref,
    *rest,
):
    mine_refs, theirs_refs, rest = rest[:SIDE], rest[SIDE:2 * SIDE], rest[2 * SIDE:]
    outs = 1 if last else 3 if first else 2
    out_ref = rest[0]
    space, total = rest[outs:outs + 2]
    span, node = place_ref[0], place_ref[1]
    row_count = total.shape[0]
    offered = listed_ref.shape[1]
    z, y, core = node // (SIDE * CORES), (node // CORES) % SIDE, node % CORES
    each = mine_refs[0].shape[0] // SIDE
    if first:
        lists = rest[outs + 2]
        lists[...] = jnp.zeros_like(lists)
        lane_block = pl.ds(pl.multiple_of((node // EXTRA) * TILE, TILE), TILE)
        wanted = lax.broadcasted_iota(jnp.int32, (EXTRA, TILE), 0) == node % EXTRA
    for refs, kind in ((mine_refs, core), (theirs_refs, 1 - core)):
        for j in range(SIDE):
            for k in range(SIDE):
                dz = jnp.where(kind == 0, j, k)
                dy = jnp.where(kind == 0, k, j)
                chip = ((z + SIDE - dz) % SIDE) * SIDE + (y + SIDE - dy) % SIDE
                start = pl.multiple_of(2 * row_count + (chip * CORES + kind) * offered, offered)
                space[pl.ds(start, offered), :] = refs[j][pl.ds(k * each, offered), :]
                if first:
                    raw = refs[j][pl.ds(k * each + offered, EXTRA), lane_block].astype(jnp.float32)
                    row = jnp.sum(jnp.where(wanted, raw, 0.0), axis=0, keepdims=True)
                    lists[pl.ds(chip, 1), :] += row
    space[pl.ds(0, row_count), :] = current_ref[...]

    @pl.when(span == 0)
    def _():
        space[pl.ds(row_count, row_count), :] = jnp.zeros((row_count, space.shape[1]), space.dtype)

    @pl.when(span > 0)
    def _():
        space[pl.ds(row_count, row_count), :] = previous_ref[...]

    total[...] = jnp.zeros_like(total)
    if first:
        wide_ref = rest[2]
        lanes = lax.broadcasted_iota(jnp.int32, (1, TILE), 1)
        shift = jnp.where(lanes >= TILE // CORES, offered, 0)
        slot_rows = lax.broadcasted_iota(jnp.int32, (CORES * offered, TILE), 0)

    ends = []
    reached = 0
    for r in range(counts_ref.shape[1] - 1):
        reached = reached + counts_ref[span, r]
        ends.append(reached)
    own_tiles = 2 * row_count // TILE
    for f in range(cols_ref.shape[1]):
        owner = sum((f >= end).astype(jnp.int32) for end in ends)
        col = cols_ref[span, f]
        if first:
            plain = lanes + TILE * (col % CORES)
            listed = lists[pl.ds(jnp.maximum(col - own_tiles, 0), 1), :].astype(jnp.int32) + shift
            target = jnp.where(col < own_tiles, plain, listed)
            selector = (slot_rows == target).astype(jnp.bfloat16)
            wide = lax.dot_general(
                tiles_ref[f], selector, (((1,), (1,)), ((), ())), preferred_element_type=jnp.float32
            ).astype(jnp.bfloat16)
            wide_ref[f] = wide
        else:
            wide = tiles_ref[f]
        slot = jnp.where(col < own_tiles, col // CORES, col - own_tiles // CORES)
        row_at = pl.ds(pl.multiple_of(owner * TILE, TILE), TILE)
        slot_at = pl.ds(pl.multiple_of(slot * CORES * offered, CORES * offered), CORES * offered)
        total[row_at, :] += jnp.dot(wide, space[slot_at, :], preferred_element_type=jnp.float32)
    half = halves_ref.shape[0] // SIDE
    distance = (span + SIDE - layer_id) % SIDE
    held = pl.ds(pl.multiple_of(distance * half, half), half)
    linear = 0.0
    for ref, kind in ((halves_ref, core), (others_ref, 1 - core)):
        columns = pl.ds(pl.multiple_of(kind * half, half), half)
        aggregate = total[:, columns].astype(jnp.bfloat16)
        linear = linear + jnp.dot(aggregate, ref[held, :], preferred_element_type=jnp.float32)
    fresh = jnp.maximum(linear, 0.0).astype(jnp.bfloat16)
    out_ref[...] = fresh
    if not last:
        rest[1][...] = offered_rows(listed_ref[...], fresh)


def place_kernel(place_ref, *refs):
    out_ref, held, in_sems, out_sems = refs[-4:]
    spans = out_ref.shape[0]
    span = place_ref[0]
    first_ref = 0
    for layer_id in range(spans):
        halved = 2 if layer_id == spans - 1 else 1
        parts = []
        for distance in range(spans):
            pieces = halved if distance == 2 else 1
            rows = held.shape[1] // pieces
            parts += [(distance, rows * i, rows) for i in range(pieces)]
        sources = refs[first_ref:first_ref + len(parts)]
        first_ref += len(parts)

        @pl.when(span == layer_id)
        def _():
            ins, outs = [], []
            for i, (distance, start, rows) in enumerate(parts):
                staged = held.at[distance, pl.ds(start, rows)]
                target = out_ref.at[(layer_id - distance) % spans, pl.ds(start, rows)]
                ins.append(pltpu.make_async_copy(sources[i], staged, in_sems.at[i]))
                outs.append(pltpu.make_async_copy(staged, target, out_sems.at[i]))
            for copy in ins:
                copy.start()
            for i in range(len(parts)):
                ins[i].wait()
                outs[i].start()
            for copy in outs:
                copy.wait()


def on_device(features, weights, boundary, pick_index, counts, tile_cols, tile_vals):
    spans, row_count, width = features.shape
    layers = lax.axis_size("layer")
    nodes = lax.axis_size("node")
    offered = boundary.shape[2]
    tile_total = tile_vals.shape[2]
    node = lax.axis_index("node")
    span = lax.axis_index("layer")
    place = jnp.stack([span, node]).astype(jnp.int32)
    current = lax.dynamic_index_in_dim(features, span, 0, keepdims=False)
    listed = lax.dynamic_index_in_dim(boundary, span, 0, keepdims=False)
    lists = lax.dynamic_index_in_dim(pick_index, span, 0, keepdims=False)[0]
    counts, tile_cols = counts[:, 0], tile_cols[:, 0]
    rows_shape = jax.ShapeDtypeStruct((row_count, width), jnp.bfloat16)
    wide_shape = jax.ShapeDtypeStruct((tile_total, TILE, CORES * offered), jnp.bfloat16)
    block_shape = jax.ShapeDtypeStruct((offered, width), jnp.bfloat16)
    params = pltpu.CompilerParams(vmem_limit_bytes=16 << 20)
    block = pl.pallas_call(
        first_kernel,
        out_shape=jax.ShapeDtypeStruct((offered + EXTRA, width), jnp.bfloat16),
        in_specs=[SMEM, VMEM, VMEM, VMEM],
        out_specs=VMEM,
        compiler_params=params,
    )(place, current, listed, lists)
    previous = lax.dynamic_index_in_dim(features, jnp.maximum(span - 1, 0), 0, keepdims=False)
    tiles = lax.dynamic_index_in_dim(tile_vals, span, 0, keepdims=False)[0]
    known = moving = None
    placed = []
    for layer_id in range(layers):
        first, last = layer_id == 0, layer_id == layers - 1
        row = jnp.concatenate([block] + [along(block, k, 0) for k in range(1, SIDE)], 0)
        if first:
            half = lax.dynamic_slice_in_dim(weights[0], (node % CORES) * (width // CORES), width // CORES, 0)
            half, row = lax.optimization_barrier((half, row))
            halves = [half]
            for distance in range(1, layers):
                halves.append(to_plane(half, [(i, (i + distance) % layers) for i in range(layers)]))
            halves = jnp.concatenate(halves, 0)
            known = [halves, other_core(halves)]
        mine = [row] + [along(row, j, 1) for j in range(1, SIDE)]
        theirs = [other_core(part) for part in mine]
        if moving is not None:
            mine, theirs, moving = lax.optimization_barrier((mine, theirs, moving))
            previous = moving[0]
            placed += [current] + moving
        scratch = [
            pltpu.VMEM((2 * row_count + nodes * offered, width), jnp.bfloat16),
            pltpu.VMEM((row_count, width), jnp.float32),
        ]
        if first:
            scratch.append(pltpu.VMEM((SIDE * SIDE, TILE), jnp.float32))
        outs = [rows_shape] if last else [rows_shape, block_shape]
        if first:
            outs.append(wide_shape)
        results = pl.pallas_call(
            functools.partial(layer_kernel, layer_id, first, last),
            out_shape=outs,
            in_specs=[SMEM, SMEM, SMEM] + [VMEM] * (6 + 2 * SIDE),
            out_specs=[VMEM] * len(outs),
            scratch_shapes=scratch,
            compiler_params=params,
        )(place, counts, tile_cols, listed, current, previous, tiles, *known, *mine, *theirs)
        current = results[0]
        if not last:
            block = results[1]
        if first:
            tiles = results[2]
        before, after, across = [(layer_id + step) % layers for step in (3, 1, 2)]
        if not last:
            moving = [
                to_plane(current, [(i, (i + 1) % layers) for i in range(layers)]),
                to_plane(current, [(across, layer_id)]),
                to_plane(current, [(after, layer_id)]),
            ]
        else:
            half = row_count // 2
            relayed = to_plane(current[:half], [(across, before)])
            placed += [
                current,
                to_plane(current, [(before, layer_id)]),
                to_plane(relayed, [(before, layer_id)]),
                to_plane(current[half:], [(across, layer_id)]),
                to_plane(current, [(after, layer_id)]),
            ]
    return pl.pallas_call(
        place_kernel,
        out_shape=jax.ShapeDtypeStruct(features.shape, features.dtype),
        in_specs=[SMEM] + [ANY] * len(placed),
        out_specs=ANY,
        scratch_shapes=[
            pltpu.VMEM(features.shape, features.dtype),
            pltpu.SemaphoreType.DMA((5,)),
            pltpu.SemaphoreType.DMA((5,)),
        ],
        compiler_params=params,
    )(place, *placed)


def solution(mesh):
    return jax.shard_map(
        on_device,
        mesh=mesh,
        in_specs=(
            P(None, "node", None),
            P("layer", None, None),
            P(None, "node", None),
            P(None, "node", None, None),
            P(None, "node", None),
            P(None, "node", None),
            P(None, "node", None, None, None),
        ),
        out_specs=P(None, "node", "layer"),
        check_vma=False,
    )
```

```python
import functools

import jax
import jax.numpy as jnp
from jax import lax
from jax.experimental import pallas as pl
from jax.experimental.pallas import tpu as pltpu
from jax.sharding import PartitionSpec as P

TILE = 128
SIDE = 4
CORES = 2
EXTRA = 16
ANY = pl.BlockSpec(memory_space=pl.ANY)
SMEM = pl.BlockSpec(memory_space=pltpu.SMEM)
VMEM = pl.BlockSpec(memory_space=pltpu.VMEM)
PLACES = [(z, y, core) for z in range(SIDE) for y in range(SIDE) for core in range(CORES)]


def node_of(z, y, core):
    return ((z % SIDE) * SIDE + y % SIDE) * CORES + core


def along(block, distance, phase):
    route = []
    for z, y, core in PLACES:
        if core == phase:
            target = node_of(z, y + distance, core)
        else:
            target = node_of(z + distance, y, core)
        route.append((node_of(z, y, core), target))
    return lax.ppermute(block, "node", route)


def other_core(block):
    route = [(node_of(z, y, core), node_of(z, y, 1 - core)) for z, y, core in PLACES]
    return lax.ppermute(block, "node", route)


def to_plane(block, pairs):
    return lax.ppermute(block, "layer", pairs)


def offered_rows(listed, rows):
    row_ids = lax.broadcasted_iota(jnp.int32, (rows.shape[0], listed.shape[1]), 0)
    selector = (row_ids == listed).astype(jnp.bfloat16)
    picked = lax.dot_general(
        selector, rows, (((0,), (0,)), ((), ())), preferred_element_type=jnp.float32
    )
    return picked.astype(jnp.bfloat16)


def first_kernel(place_ref, rows_ref, listed_ref, lists_ref, block_ref):
    node = place_ref[1]
    offered = listed_ref.shape[1]
    nodes, picks = lists_ref.shape
    block_ref[pl.ds(offered, EXTRA), :] = jnp.zeros((EXTRA, block_ref.shape[1]), jnp.bfloat16)
    lists = lists_ref[...].astype(jnp.float32).astype(jnp.bfloat16)
    for core in range(CORES):
        @pl.when(node % CORES == core)
        def _():
            for part in range(nodes // EXTRA):
                lanes = pl.ds(part * CORES * picks + core * picks, picks)
                block_ref[pl.ds(offered, EXTRA), lanes] = lists[part * EXTRA:(part + 1) * EXTRA]
    block_ref[pl.ds(0, offered), :] = offered_rows(listed_ref[...], rows_ref[...])


def layer_kernel(
    layer_id, first, last,
    place_ref, counts_ref, cols_ref, listed_ref, current_ref, previous_ref, tiles_ref, halves_ref, others_ref,
    *rest,
):
    mine_refs, theirs_refs, rest = rest[:SIDE], rest[SIDE:2 * SIDE], rest[2 * SIDE:]
    if not first:
        back_ref, *rest = rest
    outs = 1 if last else 3
    out_ref = rest[0]
    space, total = rest[outs:outs + 2]
    span, node = place_ref[0], place_ref[1]
    row_count = total.shape[0]
    offered = listed_ref.shape[1]
    z, y, core = node // (SIDE * CORES), (node // CORES) % SIDE, node % CORES
    each = mine_refs[0].shape[0] // SIDE
    if first:
        lists = rest[outs + 2]
        lists[...] = jnp.zeros_like(lists)
        lane_block = pl.ds(pl.multiple_of((node // EXTRA) * TILE, TILE), TILE)
        wanted = lax.broadcasted_iota(jnp.int32, (EXTRA, TILE), 0) == node % EXTRA
    for refs, kind in ((mine_refs, core), (theirs_refs, 1 - core)):
        for j in range(SIDE):
            for k in range(SIDE):
                dz = jnp.where(kind == 0, j, k)
                dy = jnp.where(kind == 0, k, j)
                chip = ((z + SIDE - dz) % SIDE) * SIDE + (y + SIDE - dy) % SIDE
                start = pl.multiple_of(2 * row_count + (chip * CORES + kind) * offered, offered)
                space[pl.ds(start, offered), :] = refs[j][pl.ds(k * each, offered), :]
                if first:
                    raw = refs[j][pl.ds(k * each + offered, EXTRA), lane_block].astype(jnp.float32)
                    row = jnp.sum(jnp.where(wanted, raw, 0.0), axis=0, keepdims=True)
                    lists[pl.ds(chip, 1), :] += row
    space[pl.ds(0, row_count), :] = current_ref[...]

    @pl.when(span == 0)
    def _():
        space[pl.ds(row_count, row_count), :] = jnp.zeros((row_count, space.shape[1]), space.dtype)

    @pl.when(span > 0)
    def _():
        space[pl.ds(row_count, row_count), :] = previous_ref[...]

    total[...] = jnp.zeros_like(total)
    if first:
        wide_ref = rest[2]
        lanes = lax.broadcasted_iota(jnp.int32, (1, TILE), 1)
        shift = jnp.where(lanes >= TILE // CORES, offered, 0)
        slot_rows = lax.broadcasted_iota(jnp.int32, (CORES * offered, TILE), 0)

    ends = []
    reached = 0
    for r in range(counts_ref.shape[1] - 1):
        reached = reached + counts_ref[span, r]
        ends.append(reached)
    own_tiles = 2 * row_count // TILE
    for f in range(cols_ref.shape[1]):
        owner = sum((f >= end).astype(jnp.int32) for end in ends)
        col = cols_ref[span, f]
        if first:
            plain = lanes + TILE * (col % CORES)
            listed = lists[pl.ds(jnp.maximum(col - own_tiles, 0), 1), :].astype(jnp.int32) + shift
            target = jnp.where(col < own_tiles, plain, listed)
            selector = (slot_rows == target).astype(jnp.bfloat16)
            wide = lax.dot_general(
                tiles_ref[f], selector, (((1,), (1,)), ((), ())), preferred_element_type=jnp.float32
            ).astype(jnp.bfloat16)
            wide_ref[f] = wide
        else:
            wide = tiles_ref[f]
        slot = jnp.where(col < own_tiles, col // CORES, col - own_tiles // CORES)
        row_at = pl.ds(pl.multiple_of(owner * TILE, TILE), TILE)
        slot_at = pl.ds(pl.multiple_of(slot * CORES * offered, CORES * offered), CORES * offered)
        total[row_at, :] += jnp.dot(wide, space[slot_at, :], preferred_element_type=jnp.float32)
    half = halves_ref.shape[0] // SIDE
    distance = (span + SIDE - layer_id) % SIDE
    held = pl.ds(pl.multiple_of(distance * half, half), half)
    linear = 0.0
    for ref, kind in ((halves_ref, core), (others_ref, 1 - core)):
        columns = pl.ds(pl.multiple_of(kind * half, half), half)
        aggregate = total[:, columns].astype(jnp.bfloat16)
        linear = linear + jnp.dot(aggregate, ref[held, :], preferred_element_type=jnp.float32)
    fresh = jnp.maximum(linear, 0.0).astype(jnp.bfloat16)
    out_ref[...] = fresh
    if not last:
        rest[1][...] = offered_rows(listed_ref[...], fresh)
    if not first and not last:
        moved_ref = rest[2]

        @pl.when(span == layer_id)
        def _():
            moved_ref[...] = back_ref[...]

        @pl.when(span != layer_id)
        def _():
            moved_ref[...] = fresh


def place_kernel(place_ref, *refs):
    out_ref, held, in_sems, out_sems = refs[-4:]
    spans = out_ref.shape[0]
    span = place_ref[0]
    first_ref = 0
    for layer_id in range(spans):
        halved = 2 if layer_id == spans - 1 else 1
        parts = []
        for distance in range(spans):
            pieces = halved if distance == 2 else 1
            rows = held.shape[1] // pieces
            parts += [(distance, rows * i, rows) for i in range(pieces)]
        sources = refs[first_ref:first_ref + len(parts)]
        first_ref += len(parts)

        @pl.when(span == layer_id)
        def _():
            ins, outs = [], []
            for i, (distance, start, rows) in enumerate(parts):
                staged = held.at[distance, pl.ds(start, rows)]
                target = out_ref.at[(layer_id - distance) % spans, pl.ds(start, rows)]
                ins.append(pltpu.make_async_copy(sources[i], staged, in_sems.at[i]))
                outs.append(pltpu.make_async_copy(staged, target, out_sems.at[i]))
            for copy in ins:
                copy.start()
            for i in range(len(parts)):
                ins[i].wait()
                outs[i].start()
            for copy in outs:
                copy.wait()


def on_device(features, weights, boundary, pick_index, counts, tile_cols, tile_vals):
    spans, row_count, width = features.shape
    layers = lax.axis_size("layer")
    nodes = lax.axis_size("node")
    offered = boundary.shape[2]
    tile_total = tile_vals.shape[2]
    node = lax.axis_index("node")
    span = lax.axis_index("layer")
    place = jnp.stack([span, node]).astype(jnp.int32)
    current = lax.dynamic_index_in_dim(features, span, 0, keepdims=False)
    listed = lax.dynamic_index_in_dim(boundary, span, 0, keepdims=False)
    lists = lax.dynamic_index_in_dim(pick_index, span, 0, keepdims=False)[0]
    counts, tile_cols = counts[:, 0], tile_cols[:, 0]
    rows_shape = jax.ShapeDtypeStruct((row_count, width), jnp.bfloat16)
    wide_shape = jax.ShapeDtypeStruct((tile_total, TILE, CORES * offered), jnp.bfloat16)
    block_shape = jax.ShapeDtypeStruct((offered, width), jnp.bfloat16)
    params = pltpu.CompilerParams(vmem_limit_bytes=16 << 20)
    block = pl.pallas_call(
        first_kernel,
        out_shape=jax.ShapeDtypeStruct((offered + EXTRA, width), jnp.bfloat16),
        in_specs=[SMEM, VMEM, VMEM, VMEM],
        out_specs=VMEM,
        compiler_params=params,
    )(place, current, listed, lists)
    previous = lax.dynamic_index_in_dim(features, jnp.maximum(span - 1, 0), 0, keepdims=False)
    tiles = lax.dynamic_index_in_dim(tile_vals, span, 0, keepdims=False)[0]
    known = forward = back = None
    placed = []
    for layer_id in range(layers):
        first, last = layer_id == 0, layer_id == layers - 1
        row = jnp.concatenate([block] + [along(block, k, 0) for k in range(1, SIDE)], 0)
        if first:
            half = lax.dynamic_slice_in_dim(weights[0], (node % CORES) * (width // CORES), width // CORES, 0)
            halves = [half]
            for distance in range(1, layers):
                halves.append(to_plane(half, [(i, (i + distance) % layers) for i in range(layers)]))
            halves = jnp.concatenate(halves, 0)
            known = [halves, other_core(halves)]
        mine = [row] + [along(row, j, 1) for j in range(1, SIDE)]
        theirs = [other_core(part) for part in mine]
        if back is not None:
            previous = forward
            placed.append([current, forward, None, back])
        scratch = [
            pltpu.VMEM((2 * row_count + nodes * offered, width), jnp.bfloat16),
            pltpu.VMEM((row_count, width), jnp.float32),
        ]
        if first:
            scratch.append(pltpu.VMEM((SIDE * SIDE, TILE), jnp.float32))
        outs = [rows_shape] if last else [rows_shape, block_shape]
        if first:
            outs.append(wide_shape)
        elif not last:
            outs.append(rows_shape)
        results = pl.pallas_call(
            functools.partial(layer_kernel, layer_id, first, last),
            out_shape=outs,
            in_specs=[SMEM, SMEM, SMEM] + [VMEM] * (6 + 2 * SIDE + (not first)),
            out_specs=[VMEM] * len(outs),
            scratch_shapes=scratch,
            compiler_params=params,
        )(place, counts, tile_cols, listed, current, previous, tiles, *known, *mine, *theirs, *([] if first else [back]))
        current = results[0]
        if not last:
            block = results[1]
        if first:
            tiles = results[2]
        before, after, across = [(layer_id + step) % layers for step in (3, 1, 2)]
        if not last:
            forward = to_plane(current, [(i, (i + 1) % layers) for i in range(layers)])
            pairs = [(after, layer_id), (across, after)]
            moved = current
            if not first:
                pairs.append((layer_id, before))
                moved = results[2]
            back = to_plane(moved, pairs)
            if not first:
                placed[-1][2] = back
        else:
            half = row_count // 2
            relayed = to_plane(current[:half], [(across, before)])
            placed[-1][2] = to_plane(back, [(layer_id, before)])
            placed.append([
                current,
                to_plane(current, [(before, layer_id)]),
                to_plane(relayed, [(before, layer_id)]),
                to_plane(current[half:], [(across, layer_id)]),
                to_plane(current, [(after, layer_id)]),
            ])
    placed = sum(placed, [])
    return pl.pallas_call(
        place_kernel,
        out_shape=jax.ShapeDtypeStruct(features.shape, features.dtype),
        in_specs=[SMEM] + [ANY] * len(placed),
        out_specs=ANY,
        scratch_shapes=[
            pltpu.VMEM(features.shape, features.dtype),
            pltpu.SemaphoreType.DMA((5,)),
            pltpu.SemaphoreType.DMA((5,)),
        ],
        compiler_params=params,
    )(place, *placed)


def solution(mesh):
    return jax.shard_map(
        on_device,
        mesh=mesh,
        in_specs=(
            P(None, "node", None),
            P("layer", None, None),
            P(None, "node", None),
            P(None, "node", None, None),
            P(None, "node", None),
            P(None, "node", None),
            P(None, "node", None, None, None),
        ),
        out_specs=P(None, "node", "layer"),
        check_vma=False,
    )
```

```python
import functools

import jax
import jax.numpy as jnp
from jax import lax
from jax.experimental import pallas as pl
from jax.experimental.pallas import tpu as pltpu
from jax.sharding import PartitionSpec as P

TILE = 128
SIDE = 4
CORES = 2
EXTRA = 16
ANY = pl.BlockSpec(memory_space=pl.ANY)
SMEM = pl.BlockSpec(memory_space=pltpu.SMEM)
HBM = pl.BlockSpec(memory_space=pltpu.HBM)
VMEM = pl.BlockSpec(memory_space=pltpu.VMEM)
PLACES = [(z, y, core) for z in range(SIDE) for y in range(SIDE) for core in range(CORES)]


def node_of(z, y, core):
    return ((z % SIDE) * SIDE + y % SIDE) * CORES + core


def along(block, distance, phase):
    route = []
    for z, y, core in PLACES:
        if core == phase:
            target = node_of(z, y + distance, core)
        else:
            target = node_of(z + distance, y, core)
        route.append((node_of(z, y, core), target))
    return lax.ppermute(block, "node", route)


def other_core(block):
    route = [(node_of(z, y, core), node_of(z, y, 1 - core)) for z, y, core in PLACES]
    return lax.ppermute(block, "node", route)


def to_plane(block, pairs):
    return lax.ppermute(block, "layer", pairs)


def offered_rows(listed, rows):
    row_ids = lax.broadcasted_iota(jnp.int32, (rows.shape[0], listed.shape[1]), 0)
    selector = (row_ids == listed).astype(jnp.bfloat16)
    picked = lax.dot_general(
        selector, rows, (((0,), (0,)), ((), ())), preferred_element_type=jnp.float32
    )
    return picked.astype(jnp.bfloat16)


def first_kernel(place_ref, rows_ref, listed_ref, lists_ref, block_ref):
    node = place_ref[1]
    offered = listed_ref.shape[1]
    nodes, picks = lists_ref.shape
    block_ref[pl.ds(offered, EXTRA), :] = jnp.zeros((EXTRA, block_ref.shape[1]), jnp.bfloat16)
    lists = lists_ref[...].astype(jnp.float32).astype(jnp.bfloat16)
    for core in range(CORES):
        @pl.when(node % CORES == core)
        def _():
            for part in range(nodes // EXTRA):
                lanes = pl.ds(part * CORES * picks + core * picks, picks)
                block_ref[pl.ds(offered, EXTRA), lanes] = lists[part * EXTRA:(part + 1) * EXTRA]
    block_ref[pl.ds(0, offered), :] = offered_rows(listed_ref[...], rows_ref[...])


def layer_kernel(
    layer_id, first, last,
    place_ref, counts_ref, cols_ref, listed_ref, current_ref, previous_ref, tiles_ref, halves_ref, others_ref,
    *rest,
):
    mine_refs, theirs_refs, rest = rest[:SIDE], rest[SIDE:2 * SIDE], rest[2 * SIDE:]
    if not first:
        back_ref, *rest = rest
    outs = 1 if last else 3
    out_ref = rest[0]
    space, total = rest[outs:outs + 2]
    span, node = place_ref[0], place_ref[1]
    row_count = total.shape[0]
    offered = listed_ref.shape[1]
    z, y, core = node // (SIDE * CORES), (node // CORES) % SIDE, node % CORES
    each = mine_refs[0].shape[0] // SIDE
    if first:
        lists = rest[outs + 2]
        lane_block = pl.ds(pl.multiple_of((node // EXTRA) * TILE, TILE), TILE)
        wanted = lax.broadcasted_iota(jnp.int32, (EXTRA, TILE), 0) == node % EXTRA
    for refs, kind in ((mine_refs, core), (theirs_refs, 1 - core)):
        for j in range(SIDE):
            for k in range(SIDE):
                dz = jnp.where(kind == 0, j, k)
                dy = jnp.where(kind == 0, k, j)
                chip = ((z + SIDE - dz) % SIDE) * SIDE + (y + SIDE - dy) % SIDE
                start = pl.multiple_of(2 * row_count + (chip * CORES + kind) * offered, offered)
                space[pl.ds(start, offered), :] = refs[j][pl.ds(k * each, offered), :]
                if first:
                    raw = refs[j][pl.ds(k * each + offered, EXTRA), lane_block].astype(jnp.float32)
                    row = jnp.sum(jnp.where(wanted, raw, 0.0), axis=0, keepdims=True)
                    lists[pl.ds(chip + kind * SIDE * SIDE, 1), :] = row
    space[pl.ds(0, row_count), :] = current_ref[...]

    @pl.when(span == 0)
    def _():
        space[pl.ds(row_count, row_count), :] = jnp.zeros((row_count, space.shape[1]), space.dtype)

    @pl.when(span > 0)
    def _():
        space[pl.ds(row_count, row_count), :] = previous_ref[...]

    total[...] = jnp.zeros_like(total)
    if first:
        wide_ref = rest[2]
        lanes = lax.broadcasted_iota(jnp.int32, (1, TILE), 1)
        shift = jnp.where(lanes >= TILE // CORES, offered, 0)
        slot_rows = lax.broadcasted_iota(jnp.int32, (CORES * offered, TILE), 0)

    ends = []
    reached = 0
    for r in range(counts_ref.shape[1] - 1):
        reached = reached + counts_ref[span, r]
        ends.append(reached)
    own_tiles = 2 * row_count // TILE
    for f in range(cols_ref.shape[1]):
        owner = sum((f >= end).astype(jnp.int32) for end in ends)
        col = cols_ref[span, f]
        if first:
            plain = lanes + TILE * (col % CORES)
            chip = jnp.maximum(col - own_tiles, 0)
            listed = lists[pl.ds(chip, 1), :] + lists[pl.ds(chip + SIDE * SIDE, 1), :]
            listed = listed.astype(jnp.int32) + shift
            target = jnp.where(col < own_tiles, plain, listed)
            selector = (slot_rows == target).astype(jnp.bfloat16)
            wide = lax.dot_general(
                tiles_ref[f], selector, (((1,), (1,)), ((), ())), preferred_element_type=jnp.float32
            ).astype(jnp.bfloat16)
            wide_ref[f] = wide
        else:
            wide = tiles_ref[f]
        slot = jnp.where(col < own_tiles, col // CORES, col - own_tiles // CORES)
        row_at = pl.ds(pl.multiple_of(owner * TILE, TILE), TILE)
        slot_at = pl.ds(pl.multiple_of(slot * CORES * offered, CORES * offered), CORES * offered)
        total[row_at, :] += jnp.dot(wide, space[slot_at, :], preferred_element_type=jnp.float32)
    half = halves_ref.shape[0] // SIDE
    distance = (span + SIDE - layer_id) % SIDE
    held = pl.ds(pl.multiple_of(distance * half, half), half)
    linear = 0.0
    for ref, kind in ((halves_ref, core), (others_ref, 1 - core)):
        columns = pl.ds(pl.multiple_of(kind * half, half), half)
        aggregate = total[:, columns].astype(jnp.bfloat16)
        linear = linear + jnp.dot(aggregate, ref[held, :], preferred_element_type=jnp.float32)
    fresh = jnp.maximum(linear, 0.0).astype(jnp.bfloat16)
    out_ref[...] = fresh
    if not last:
        rest[1][...] = offered_rows(listed_ref[...], fresh)
    if not first and not last:
        moved_ref = rest[2]

        @pl.when(span == layer_id)
        def _():
            moved_ref[...] = back_ref[...]

        @pl.when(span != layer_id)
        def _():
            moved_ref[...] = fresh


def place_kernel(*refs):
    out_ref, sems = refs[-2:]
    spans = out_ref.shape[0]
    span = lax.axis_index("layer")
    first_ref = 0
    for layer_id in range(spans):
        parts = [0, 1, 2, 2, 3] if layer_id == spans - 1 else list(range(spans))
        sources = refs[first_ref:first_ref + len(parts)]
        first_ref += len(parts)

        @pl.when(span == layer_id)
        def _():
            copies, start = [], 0
            for i, (distance, source) in enumerate(zip(parts, sources)):
                rows = source.shape[0]
                target = out_ref.at[(layer_id - distance) % spans, pl.ds(start % out_ref.shape[1], rows)]
                start += rows
                copies.append(pltpu.make_async_copy(source, target, sems.at[i]))
            for copy in copies:
                copy.start()
            for copy in copies:
                copy.wait()


def on_device(features, weights, boundary, pick_index, counts, tile_cols, tile_vals):
    spans, row_count, width = features.shape
    layers = lax.axis_size("layer")
    nodes = lax.axis_size("node")
    offered = boundary.shape[2]
    tile_total = tile_vals.shape[2]
    node = lax.axis_index("node")
    span = lax.axis_index("layer")
    place = jnp.stack([span, node]).astype(jnp.int32)
    current = lax.dynamic_index_in_dim(features, span, 0, keepdims=False)
    listed = lax.dynamic_index_in_dim(boundary, span, 0, keepdims=False)
    lists = lax.dynamic_index_in_dim(pick_index, span, 0, keepdims=False)[0]
    counts, tile_cols = counts[:, 0], tile_cols[:, 0]
    rows_shape = jax.ShapeDtypeStruct((row_count, width), jnp.bfloat16)
    wide_shape = jax.ShapeDtypeStruct((tile_total, TILE, CORES * offered), jnp.bfloat16)
    block_shape = jax.ShapeDtypeStruct((offered, width), jnp.bfloat16)
    params = pltpu.CompilerParams(vmem_limit_bytes=16 << 20)
    block = pl.pallas_call(
        first_kernel,
        out_shape=jax.ShapeDtypeStruct((offered + EXTRA, width), jnp.bfloat16),
        in_specs=[SMEM, VMEM, VMEM, VMEM],
        out_specs=VMEM,
        compiler_params=params,
    )(place, current, listed, lists)
    previous = lax.dynamic_index_in_dim(features, jnp.maximum(span - 1, 0), 0, keepdims=False)
    tiles = lax.dynamic_index_in_dim(tile_vals, span, 0, keepdims=False)[0]
    known = forward = back = None
    placed = []
    for layer_id in range(layers):
        first, last = layer_id == 0, layer_id == layers - 1
        row = jnp.concatenate([block] + [along(block, k, 0) for k in range(1, SIDE)], 0)
        if first:
            half = lax.dynamic_slice_in_dim(weights[0], (node % CORES) * (width // CORES), width // CORES, 0)
            halves = [half]
            for distance in range(1, layers):
                halves.append(to_plane(half, [(i, (i + distance) % layers) for i in range(layers)]))
            halves = jnp.concatenate(halves, 0)
            known = [halves, other_core(halves)]
        mine = [row] + [along(row, j, 1) for j in range(1, SIDE)]
        theirs = [other_core(part) for part in mine]
        if back is not None:
            previous = forward
            placed.append([current, forward, None, back])
        scratch = [
            pltpu.VMEM((2 * row_count + nodes * offered, width), jnp.bfloat16),
            pltpu.VMEM((row_count, width), jnp.float32),
        ]
        if first:
            scratch.append(pltpu.VMEM((CORES * SIDE * SIDE, TILE), jnp.float32))
        outs = [rows_shape] if last else [rows_shape, block_shape]
        if first:
            outs.append(wide_shape)
        elif not last:
            outs.append(rows_shape)
        results = pl.pallas_call(
            functools.partial(layer_kernel, layer_id, first, last),
            out_shape=outs,
            in_specs=[SMEM, SMEM, SMEM] + [VMEM] * (6 + 2 * SIDE + (not first)),
            out_specs=[VMEM] * len(outs),
            scratch_shapes=scratch,
            compiler_params=params,
        )(place, counts, tile_cols, listed, current, previous, tiles, *known, *mine, *theirs, *([] if first else [back]))
        current = results[0]
        if not last:
            block = results[1]
        if first:
            tiles = results[2]
        before, after, across = [(layer_id + step) % layers for step in (3, 1, 2)]
        if not last:
            forward = to_plane(current, [(i, (i + 1) % layers) for i in range(layers)])
            pairs = [(after, layer_id), (across, after)]
            moved = current
            if not first:
                pairs.append((layer_id, before))
                moved = results[2]
            back = to_plane(moved, pairs)
            if not first:
                placed[-1][2] = back
        else:
            half = row_count // 2
            relayed = to_plane(current[:half], [(across, before)])
            placed[-1][2] = to_plane(back, [(layer_id, before)])
            placed.append([
                current,
                to_plane(current, [(before, layer_id)]),
                to_plane(relayed, [(before, layer_id)]),
                to_plane(current[half:], [(across, layer_id)]),
                to_plane(current, [(after, layer_id)]),
            ])
    placed = sum(placed, [])
    return pl.pallas_call(
        place_kernel,
        out_shape=jax.ShapeDtypeStruct(features.shape, features.dtype),
        in_specs=[VMEM] * len(placed),
        out_specs=HBM,
        scratch_shapes=[pltpu.SemaphoreType.DMA((5,))],
        compiler_params=params,
    )(*placed)


def solution(mesh):
    return jax.shard_map(
        on_device,
        mesh=mesh,
        in_specs=(
            P(None, "node", None),
            P("layer", None, None),
            P(None, "node", None),
            P(None, "node", None, None),
            P(None, "node", None),
            P(None, "node", None),
            P(None, "node", None, None, None),
        ),
        out_specs=P(None, "node", "layer"),
        check_vma=False,
    )
```

```python
import functools

import jax
import jax.numpy as jnp
from jax import lax
from jax.experimental import pallas as pl
from jax.experimental.pallas import tpu as pltpu
from jax.sharding import PartitionSpec as P

TILE = 128
SIDE = 4
CORES = 2
EXTRA = 16
ANY = pl.BlockSpec(memory_space=pl.ANY)
SMEM = pl.BlockSpec(memory_space=pltpu.SMEM)
HBM = pl.BlockSpec(memory_space=pltpu.HBM)
VMEM = pl.BlockSpec(memory_space=pltpu.VMEM)
PLACES = [(z, y, core) for z in range(SIDE) for y in range(SIDE) for core in range(CORES)]


def node_of(z, y, core):
    return ((z % SIDE) * SIDE + y % SIDE) * CORES + core


def along(block, distance, phase):
    route = []
    for z, y, core in PLACES:
        if core == phase:
            target = node_of(z, y + distance, core)
        else:
            target = node_of(z + distance, y, core)
        route.append((node_of(z, y, core), target))
    return lax.ppermute(block, "node", route)


def other_core(block):
    route = [(node_of(z, y, core), node_of(z, y, 1 - core)) for z, y, core in PLACES]
    return lax.ppermute(block, "node", route)


def to_plane(block, pairs):
    return lax.ppermute(block, "layer", pairs)


def offered_rows(listed, rows):
    row_ids = lax.broadcasted_iota(jnp.int32, (rows.shape[0], listed.shape[1]), 0)
    selector = (row_ids == listed).astype(jnp.bfloat16)
    picked = lax.dot_general(
        selector, rows, (((0,), (0,)), ((), ())), preferred_element_type=jnp.float32
    )
    return picked.astype(jnp.bfloat16)


def first_kernel(place_ref, rows_ref, listed_ref, lists_ref, block_ref):
    span, node = place_ref[0], place_ref[1]
    offered = listed_ref.shape[2]
    nodes, picks = lists_ref.shape[2:]
    block_ref[pl.ds(offered, EXTRA), :] = jnp.zeros((EXTRA, block_ref.shape[1]), jnp.bfloat16)
    lists = lists_ref[span, 0].astype(jnp.float32).astype(jnp.bfloat16)
    for core in range(CORES):
        @pl.when(node % CORES == core)
        def _():
            for part in range(nodes // EXTRA):
                lanes = pl.ds(part * CORES * picks + core * picks, picks)
                block_ref[pl.ds(offered, EXTRA), lanes] = lists[part * EXTRA:(part + 1) * EXTRA]
    block_ref[pl.ds(0, offered), :] = offered_rows(listed_ref[span], rows_ref[...])


def layer_kernel(
    layer_id, first, last,
    place_ref, counts_ref, cols_ref, listed_ref, current_ref, previous_ref, tiles_ref, halves_ref, others_ref,
    *rest,
):
    mine_refs, theirs_refs, rest = rest[:SIDE], rest[SIDE:2 * SIDE], rest[2 * SIDE:]
    if not first:
        back_ref, *rest = rest
    outs = 1 if last else 3
    out_ref = rest[0]
    space, total = rest[outs:outs + 2]
    span, node = place_ref[0], place_ref[1]
    row_count = total.shape[0]
    offered = listed_ref.shape[2]
    z, y, core = node // (SIDE * CORES), (node // CORES) % SIDE, node % CORES
    each = mine_refs[0].shape[0] // SIDE
    if first:
        lists = rest[outs + 2]
        lane_block = pl.ds(pl.multiple_of((node // EXTRA) * TILE, TILE), TILE)
        wanted = lax.broadcasted_iota(jnp.int32, (EXTRA, TILE), 0) == node % EXTRA
    for refs, kind in ((mine_refs, core), (theirs_refs, 1 - core)):
        for j in range(SIDE):
            for k in range(SIDE):
                dz = jnp.where(kind == 0, j, k)
                dy = jnp.where(kind == 0, k, j)
                chip = ((z + SIDE - dz) % SIDE) * SIDE + (y + SIDE - dy) % SIDE
                start = pl.multiple_of(2 * row_count + (chip * CORES + kind) * offered, offered)
                space[pl.ds(start, offered), :] = refs[j][pl.ds(k * each, offered), :]
                if first:
                    raw = refs[j][pl.ds(k * each + offered, EXTRA), lane_block].astype(jnp.float32)
                    row = jnp.sum(jnp.where(wanted, raw, 0.0), axis=0, keepdims=True)
                    lists[pl.ds(chip + kind * SIDE * SIDE, 1), :] = row
    space[pl.ds(0, row_count), :] = current_ref[...]

    @pl.when(span == 0)
    def _():
        space[pl.ds(row_count, row_count), :] = jnp.zeros((row_count, space.shape[1]), space.dtype)

    @pl.when(span > 0)
    def _():
        space[pl.ds(row_count, row_count), :] = previous_ref[...]

    total[...] = jnp.zeros_like(total)
    if first:
        wide_ref = rest[2]
        lanes = lax.broadcasted_iota(jnp.int32, (1, TILE), 1)
        shift = jnp.where(lanes >= TILE // CORES, offered, 0)
        slot_rows = lax.broadcasted_iota(jnp.int32, (CORES * offered, TILE), 0)

    ends = []
    reached = 0
    for r in range(counts_ref.shape[1] - 1):
        reached = reached + counts_ref[span, r]
        ends.append(reached)
    own_tiles = 2 * row_count // TILE
    for f in range(cols_ref.shape[1]):
        owner = sum((f >= end).astype(jnp.int32) for end in ends)
        col = cols_ref[span, f]
        if first:
            plain = lanes + TILE * (col % CORES)
            chip = jnp.maximum(col - own_tiles, 0)
            listed = lists[pl.ds(chip, 1), :] + lists[pl.ds(chip + SIDE * SIDE, 1), :]
            listed = listed.astype(jnp.int32) + shift
            target = jnp.where(col < own_tiles, plain, listed)
            selector = (slot_rows == target).astype(jnp.bfloat16)
            wide = lax.dot_general(
                tiles_ref[f], selector, (((1,), (1,)), ((), ())), preferred_element_type=jnp.float32
            ).astype(jnp.bfloat16)
            wide_ref[f] = wide
        else:
            wide = tiles_ref[f]
        slot = jnp.where(col < own_tiles, col // CORES, col - own_tiles // CORES)
        row_at = pl.ds(pl.multiple_of(owner * TILE, TILE), TILE)
        slot_at = pl.ds(pl.multiple_of(slot * CORES * offered, CORES * offered), CORES * offered)
        total[row_at, :] += jnp.dot(wide, space[slot_at, :], preferred_element_type=jnp.float32)
    half = halves_ref.shape[0] // SIDE
    distance = (span + SIDE - layer_id) % SIDE
    held = pl.ds(pl.multiple_of(distance * half, half), half)
    linear = 0.0
    for ref, kind in ((halves_ref, core), (others_ref, 1 - core)):
        columns = pl.ds(pl.multiple_of(kind * half, half), half)
        aggregate = total[:, columns].astype(jnp.bfloat16)
        linear = linear + jnp.dot(aggregate, ref[held, :], preferred_element_type=jnp.float32)
    fresh = jnp.maximum(linear, 0.0).astype(jnp.bfloat16)
    out_ref[...] = fresh
    if not last:
        rest[1][...] = offered_rows(listed_ref[span], fresh)
    if not first and not last:
        moved_ref = rest[2]

        @pl.when(span == layer_id)
        def _():
            moved_ref[...] = back_ref[...]

        @pl.when(span != layer_id)
        def _():
            moved_ref[...] = fresh


def place_kernel(*refs):
    out_ref, sems = refs[-2:]
    spans = out_ref.shape[0]
    span = lax.axis_index("layer")
    first_ref = 0
    for layer_id in range(spans):
        parts = [0, 1, 2, 2, 3] if layer_id == spans - 1 else list(range(spans))
        sources = refs[first_ref:first_ref + len(parts)]
        first_ref += len(parts)

        @pl.when(span == layer_id)
        def _():
            copies, start = [], 0
            for i, (distance, source) in enumerate(zip(parts, sources)):
                rows = source.shape[0]
                target = out_ref.at[(layer_id - distance) % spans, pl.ds(start % out_ref.shape[1], rows)]
                start += rows
                copies.append(pltpu.make_async_copy(source, target, sems.at[i]))
            for copy in copies:
                copy.start()
            for copy in copies:
                copy.wait()


def on_device(features, weights, boundary, pick_index, counts, tile_cols, tile_vals):
    spans, row_count, width = features.shape
    layers = lax.axis_size("layer")
    nodes = lax.axis_size("node")
    offered = boundary.shape[2]
    tile_total = tile_vals.shape[2]
    node = lax.axis_index("node")
    span = lax.axis_index("layer")
    place = jnp.stack([span, node]).astype(jnp.int32)
    current = lax.dynamic_index_in_dim(features, span, 0, keepdims=False)
    counts, tile_cols = counts[:, 0], tile_cols[:, 0]
    rows_shape = jax.ShapeDtypeStruct((row_count, width), jnp.bfloat16)
    wide_shape = jax.ShapeDtypeStruct((tile_total, TILE, CORES * offered), jnp.bfloat16)
    block_shape = jax.ShapeDtypeStruct((offered, width), jnp.bfloat16)
    params = pltpu.CompilerParams(vmem_limit_bytes=16 << 20)
    block = pl.pallas_call(
        first_kernel,
        out_shape=jax.ShapeDtypeStruct((offered + EXTRA, width), jnp.bfloat16),
        in_specs=[SMEM, VMEM, VMEM, VMEM],
        out_specs=VMEM,
        compiler_params=params,
    )(place, current, boundary, pick_index)
    previous = lax.dynamic_index_in_dim(features, jnp.maximum(span - 1, 0), 0, keepdims=False)
    tiles = lax.dynamic_index_in_dim(tile_vals, span, 0, keepdims=False)[0]
    known = forward = back = None
    placed = []
    for layer_id in range(layers):
        first, last = layer_id == 0, layer_id == layers - 1
        row = jnp.concatenate([block] + [along(block, k, 0) for k in range(1, SIDE)], 0)
        if first:
            half = lax.dynamic_slice_in_dim(weights[0], (node % CORES) * (width // CORES), width // CORES, 0)
            halves = [half]
            for distance in range(1, layers):
                halves.append(to_plane(half, [(i, (i + distance) % layers) for i in range(layers)]))
            halves = jnp.concatenate(halves, 0)
            known = [halves, other_core(halves)]
        mine = [row] + [along(row, j, 1) for j in range(1, SIDE)]
        theirs = [other_core(part) for part in mine]
        if back is not None:
            previous = forward
            placed.append([current, forward, None, back])
        scratch = [
            pltpu.VMEM((2 * row_count + nodes * offered, width), jnp.bfloat16),
            pltpu.VMEM((row_count, width), jnp.float32),
        ]
        if first:
            scratch.append(pltpu.VMEM((CORES * SIDE * SIDE, TILE), jnp.float32))
        outs = [rows_shape] if last else [rows_shape, block_shape]
        if first:
            outs.append(wide_shape)
        elif not last:
            outs.append(rows_shape)
        results = pl.pallas_call(
            functools.partial(layer_kernel, layer_id, first, last),
            out_shape=outs,
            in_specs=[SMEM, SMEM, SMEM] + [VMEM] * (6 + 2 * SIDE + (not first)),
            out_specs=[VMEM] * len(outs),
            scratch_shapes=scratch,
            compiler_params=params,
        )(place, counts, tile_cols, boundary, current, previous, tiles, *known, *mine, *theirs, *([] if first else [back]))
        current = results[0]
        if not last:
            block = results[1]
        if first:
            tiles = results[2]
        before, after, across = [(layer_id + step) % layers for step in (3, 1, 2)]
        if not last:
            forward = to_plane(current, [(i, (i + 1) % layers) for i in range(layers)])
            pairs = [(after, layer_id), (across, after)]
            moved = current
            if not first:
                pairs.append((layer_id, before))
                moved = results[2]
            back = to_plane(moved, pairs)
            if not first:
                placed[-1][2] = back
        else:
            half = row_count // 2
            relayed = to_plane(current[:half], [(across, before)])
            placed[-1][2] = to_plane(back, [(layer_id, before)])
            placed.append([
                current,
                to_plane(current, [(before, layer_id)]),
                to_plane(relayed, [(before, layer_id)]),
                to_plane(current[half:], [(across, layer_id)]),
                to_plane(current, [(after, layer_id)]),
            ])
    placed = sum(placed, [])
    return pl.pallas_call(
        place_kernel,
        out_shape=jax.ShapeDtypeStruct(features.shape, features.dtype),
        in_specs=[VMEM] * len(placed),
        out_specs=HBM,
        scratch_shapes=[pltpu.SemaphoreType.DMA((5,))],
        compiler_params=params,
    )(*placed)


def solution(mesh):
    return jax.shard_map(
        on_device,
        mesh=mesh,
        in_specs=(
            P(None, "node", None),
            P("layer", None, None),
            P(None, "node", None),
            P(None, "node", None, None),
            P(None, "node", None),
            P(None, "node", None),
            P(None, "node", None, None, None),
        ),
        out_specs=P(None, "node", "layer"),
        check_vma=False,
    )
```

```python
import functools

import jax
import jax.numpy as jnp
from jax import lax
from jax.experimental import pallas as pl
from jax.experimental.pallas import tpu as pltpu
from jax.sharding import PartitionSpec as P

TILE = 128
SIDE = 4
CORES = 2
EXTRA = 16
ANY = pl.BlockSpec(memory_space=pl.ANY)
SMEM = pl.BlockSpec(memory_space=pltpu.SMEM)
HBM = pl.BlockSpec(memory_space=pltpu.HBM)
VMEM = pl.BlockSpec(memory_space=pltpu.VMEM)
PLACES = [(z, y, core) for z in range(SIDE) for y in range(SIDE) for core in range(CORES)]


def node_of(z, y, core):
    return ((z % SIDE) * SIDE + y % SIDE) * CORES + core


def along(block, distance, phase):
    route = []
    for z, y, core in PLACES:
        if core == phase:
            target = node_of(z, y + distance, core)
        else:
            target = node_of(z + distance, y, core)
        route.append((node_of(z, y, core), target))
    return lax.ppermute(block, "node", route)


def other_core(block):
    route = [(node_of(z, y, core), node_of(z, y, 1 - core)) for z, y, core in PLACES]
    return lax.ppermute(block, "node", route)


def to_plane(block, pairs):
    return lax.ppermute(block, "layer", pairs)


def offered_rows(listed, rows):
    row_ids = lax.broadcasted_iota(jnp.int32, (rows.shape[0], listed.shape[1]), 0)
    selector = (row_ids == listed).astype(jnp.bfloat16)
    picked = lax.dot_general(
        selector, rows, (((0,), (0,)), ((), ())), preferred_element_type=jnp.float32
    )
    return picked.astype(jnp.bfloat16)


def first_kernel(place_ref, rows_ref, listed_ref, lists_ref, block_ref):
    span, node = place_ref[0], place_ref[1]
    offered = listed_ref.shape[2]
    nodes, picks = lists_ref.shape[2:]
    block_ref[pl.ds(offered, EXTRA), :] = jnp.zeros((EXTRA, block_ref.shape[1]), jnp.bfloat16)
    lists = lists_ref[span, 0].astype(jnp.float32).astype(jnp.bfloat16)
    for core in range(CORES):
        @pl.when(node % CORES == core)
        def _():
            for part in range(nodes // EXTRA):
                lanes = pl.ds(part * CORES * picks + core * picks, picks)
                block_ref[pl.ds(offered, EXTRA), lanes] = lists[part * EXTRA:(part + 1) * EXTRA]
    block_ref[pl.ds(0, offered), :] = offered_rows(listed_ref[span], rows_ref[...])


def selector_kernel(place_ref, listed_ref, selector_ref):
    listed = listed_ref[place_ref[0]]
    row_ids = lax.broadcasted_iota(jnp.int32, (selector_ref.shape[1], listed.shape[1]), 0)
    selector = (row_ids == listed).astype(jnp.float32)
    selector_ref[...] = jnp.transpose(selector).astype(jnp.bfloat16)


def layer_kernel(
    layer_id, first, last,
    place_ref, counts_ref, cols_ref, listed_ref, current_ref, previous_ref, tiles_ref, halves_ref, others_ref,
    *rest,
):
    mine_refs, theirs_refs, rest = rest[:SIDE], rest[SIDE:2 * SIDE], rest[2 * SIDE:]
    if not first:
        back_ref, *rest = rest
    outs = 1 if last else 3
    out_ref = rest[0]
    space, total = rest[outs:outs + 2]
    span, node = place_ref[0], place_ref[1]
    row_count = total.shape[0]
    offered = listed_ref.shape[0]
    z, y, core = node // (SIDE * CORES), (node // CORES) % SIDE, node % CORES
    each = mine_refs[0].shape[0] // SIDE
    if first:
        lists = rest[outs + 2]
        lane_block = pl.ds(pl.multiple_of((node // EXTRA) * TILE, TILE), TILE)
        wanted = lax.broadcasted_iota(jnp.int32, (EXTRA, TILE), 0) == node % EXTRA
    for refs, kind in ((mine_refs, core), (theirs_refs, 1 - core)):
        for j in range(SIDE):
            for k in range(SIDE):
                dz = jnp.where(kind == 0, j, k)
                dy = jnp.where(kind == 0, k, j)
                chip = ((z + SIDE - dz) % SIDE) * SIDE + (y + SIDE - dy) % SIDE
                start = pl.multiple_of(2 * row_count + (chip * CORES + kind) * offered, offered)
                space[pl.ds(start, offered), :] = refs[j][pl.ds(k * each, offered), :]
                if first:
                    raw = refs[j][pl.ds(k * each + offered, EXTRA), lane_block].astype(jnp.float32)
                    row = jnp.sum(jnp.where(wanted, raw, 0.0), axis=0, keepdims=True)
                    lists[pl.ds(chip + kind * SIDE * SIDE, 1), :] = row
    space[pl.ds(0, row_count), :] = current_ref[...]

    @pl.when(span == 0)
    def _():
        space[pl.ds(row_count, row_count), :] = jnp.zeros((row_count, space.shape[1]), space.dtype)

    @pl.when(span > 0)
    def _():
        space[pl.ds(row_count, row_count), :] = previous_ref[...]

    if first:
        wide_ref = rest[2]
        lanes = lax.broadcasted_iota(jnp.int32, (1, TILE), 1)
        shift = jnp.where(lanes >= TILE // CORES, offered, 0)
        slot_rows = lax.broadcasted_iota(jnp.int32, (CORES * offered, TILE), 0)

    ends = []
    reached = 0
    for r in range(counts_ref.shape[1] - 1):
        reached = reached + counts_ref[span, r]
        ends.append(reached)
    own_tiles = 2 * row_count // TILE
    begins = [0] + ends
    for f in range(cols_ref.shape[1]):
        owner = sum((f >= end).astype(jnp.int32) for end in ends)
        col = cols_ref[span, f]
        if first:
            plain = lanes + TILE * (col % CORES)
            chip = jnp.maximum(col - own_tiles, 0)
            listed = lists[pl.ds(chip, 1), :] + lists[pl.ds(chip + SIDE * SIDE, 1), :]
            listed = listed.astype(jnp.int32) + shift
            target = jnp.where(col < own_tiles, plain, listed)
            selector = (slot_rows == target).astype(jnp.bfloat16)
            wide = lax.dot_general(
                tiles_ref[f], selector, (((1,), (1,)), ((), ())), preferred_element_type=jnp.float32
            ).astype(jnp.bfloat16)
            wide_ref[f] = wide
        else:
            wide = tiles_ref[f]
        slot = jnp.where(col < own_tiles, col // CORES, col - own_tiles // CORES)
        row_at = pl.ds(pl.multiple_of(owner * TILE, TILE), TILE)
        slot_at = pl.ds(pl.multiple_of(slot * CORES * offered, CORES * offered), CORES * offered)
        product = jnp.dot(wide, space[slot_at, :], preferred_element_type=jnp.float32)
        opens = functools.reduce(jnp.logical_or, [f == begin for begin in begins])
        total[row_at, :] = jnp.where(opens, product, total[row_at, :] + product)
    half = halves_ref.shape[0] // SIDE
    distance = (span + SIDE - layer_id) % SIDE
    held = pl.ds(pl.multiple_of(distance * half, half), half)
    linear = 0.0
    for ref, kind in ((halves_ref, core), (others_ref, 1 - core)):
        columns = pl.ds(pl.multiple_of(kind * half, half), half)
        aggregate = total[:, columns].astype(jnp.bfloat16)
        linear = linear + jnp.dot(aggregate, ref[held, :], preferred_element_type=jnp.float32)
    fresh = jnp.maximum(linear, 0.0).astype(jnp.bfloat16)
    out_ref[...] = fresh
    if not last:
        picked = jnp.dot(listed_ref[...], fresh, preferred_element_type=jnp.float32)
        rest[1][...] = picked.astype(jnp.bfloat16)
    if not first and not last:
        moved_ref = rest[2]

        @pl.when(span == layer_id)
        def _():
            moved_ref[...] = back_ref[...]

        @pl.when(span != layer_id)
        def _():
            moved_ref[...] = fresh


def place_kernel(*refs):
    out_ref, sems = refs[-2:]
    spans = out_ref.shape[0]
    span = lax.axis_index("layer")
    first_ref = 0
    for layer_id in range(spans):
        parts = [0, 1, 2, 2, 3] if layer_id == spans - 1 else list(range(spans))
        sources = refs[first_ref:first_ref + len(parts)]
        first_ref += len(parts)

        @pl.when(span == layer_id)
        def _():
            copies, start = [], 0
            for i, (distance, source) in enumerate(zip(parts, sources)):
                rows = source.shape[0]
                target = out_ref.at[(layer_id - distance) % spans, pl.ds(start % out_ref.shape[1], rows)]
                start += rows
                copies.append(pltpu.make_async_copy(source, target, sems.at[i]))
            for copy in copies:
                copy.start()
            for copy in copies:
                copy.wait()


def on_device(features, weights, boundary, pick_index, counts, tile_cols, tile_vals):
    spans, row_count, width = features.shape
    layers = lax.axis_size("layer")
    nodes = lax.axis_size("node")
    offered = boundary.shape[2]
    tile_total = tile_vals.shape[2]
    node = lax.axis_index("node")
    span = lax.axis_index("layer")
    place = jnp.stack([span, node]).astype(jnp.int32)
    current = lax.dynamic_index_in_dim(features, span, 0, keepdims=False)
    selector = pl.pallas_call(
        selector_kernel,
        out_shape=jax.ShapeDtypeStruct((offered, row_count), jnp.bfloat16),
        in_specs=[SMEM, VMEM],
        out_specs=VMEM,
        compiler_params=pltpu.CompilerParams(vmem_limit_bytes=16 << 20),
    )(place, boundary)
    counts, tile_cols = counts[:, 0], tile_cols[:, 0]
    rows_shape = jax.ShapeDtypeStruct((row_count, width), jnp.bfloat16)
    wide_shape = jax.ShapeDtypeStruct((tile_total, TILE, CORES * offered), jnp.bfloat16)
    block_shape = jax.ShapeDtypeStruct((offered, width), jnp.bfloat16)
    params = pltpu.CompilerParams(vmem_limit_bytes=16 << 20)
    block = pl.pallas_call(
        first_kernel,
        out_shape=jax.ShapeDtypeStruct((offered + EXTRA, width), jnp.bfloat16),
        in_specs=[SMEM, VMEM, VMEM, VMEM],
        out_specs=VMEM,
        compiler_params=params,
    )(place, current, boundary, pick_index)
    previous = lax.dynamic_index_in_dim(features, jnp.maximum(span - 1, 0), 0, keepdims=False)
    tiles = lax.dynamic_index_in_dim(tile_vals, span, 0, keepdims=False)[0]
    known = forward = back = None
    placed = []
    for layer_id in range(layers):
        first, last = layer_id == 0, layer_id == layers - 1
        row = jnp.concatenate([block] + [along(block, k, 0) for k in range(1, SIDE)], 0)
        if first:
            half = lax.dynamic_slice_in_dim(weights[0], (node % CORES) * (width // CORES), width // CORES, 0)
            halves = [half]
            for distance in range(1, layers):
                halves.append(to_plane(half, [(i, (i + distance) % layers) for i in range(layers)]))
            halves = jnp.concatenate(halves, 0)
            known = [halves, other_core(halves)]
        mine = [row] + [along(row, j, 1) for j in range(1, SIDE)]
        theirs = [other_core(part) for part in mine]
        if back is not None:
            previous = forward
            placed.append([current, forward, None, back])
        scratch = [
            pltpu.VMEM((2 * row_count + nodes * offered, width), jnp.bfloat16),
            pltpu.VMEM((row_count, width), jnp.float32),
        ]
        if first:
            scratch.append(pltpu.VMEM((CORES * SIDE * SIDE, TILE), jnp.float32))
        outs = [rows_shape] if last else [rows_shape, block_shape]
        if first:
            outs.append(wide_shape)
        elif not last:
            outs.append(rows_shape)
        results = pl.pallas_call(
            functools.partial(layer_kernel, layer_id, first, last),
            out_shape=outs,
            in_specs=[SMEM, SMEM, SMEM] + [VMEM] * (6 + 2 * SIDE + (not first)),
            out_specs=[VMEM] * len(outs),
            scratch_shapes=scratch,
            compiler_params=params,
        )(place, counts, tile_cols, selector, current, previous, tiles, *known, *mine, *theirs, *([] if first else [back]))
        current = results[0]
        if not last:
            block = results[1]
        if first:
            tiles = results[2]
        before, after, across = [(layer_id + step) % layers for step in (3, 1, 2)]
        if not last:
            forward = to_plane(current, [(i, (i + 1) % layers) for i in range(layers)])
            pairs = [(after, layer_id), (across, after)]
            moved = current
            if not first:
                pairs.append((layer_id, before))
                moved = results[2]
            back = to_plane(moved, pairs)
            if not first:
                placed[-1][2] = back
        else:
            half = row_count // 2
            relayed = to_plane(current[:half], [(across, before)])
            placed[-1][2] = to_plane(back, [(layer_id, before)])
            placed.append([
                current,
                to_plane(current, [(before, layer_id)]),
                to_plane(relayed, [(before, layer_id)]),
                to_plane(current[half:], [(across, layer_id)]),
                to_plane(current, [(after, layer_id)]),
            ])
    placed = sum(placed, [])
    return pl.pallas_call(
        place_kernel,
        out_shape=jax.ShapeDtypeStruct(features.shape, features.dtype),
        in_specs=[VMEM] * len(placed),
        out_specs=HBM,
        scratch_shapes=[pltpu.SemaphoreType.DMA((5,))],
        compiler_params=params,
    )(*placed)


def solution(mesh):
    return jax.shard_map(
        on_device,
        mesh=mesh,
        in_specs=(
            P(None, "node", None),
            P("layer", None, None),
            P(None, "node", None),
            P(None, "node", None, None),
            P(None, "node", None),
            P(None, "node", None),
            P(None, "node", None, None, None),
        ),
        out_specs=P(None, "node", "layer"),
        check_vma=False,
    )
```

```python
import functools

import jax
import jax.numpy as jnp
from jax import lax
from jax.experimental import pallas as pl
from jax.experimental.pallas import tpu as pltpu
from jax.sharding import PartitionSpec as P

TILE = 128
SIDE = 4
CORES = 2
EXTRA = 16
PIECES = 4
ANY = pl.BlockSpec(memory_space=pl.ANY)
SMEM = pl.BlockSpec(memory_space=pltpu.SMEM)
HBM = pl.BlockSpec(memory_space=pltpu.HBM)
VMEM = pl.BlockSpec(memory_space=pltpu.VMEM)
PLACES = [(z, y, core) for z in range(SIDE) for y in range(SIDE) for core in range(CORES)]


def node_of(z, y, core):
    return ((z % SIDE) * SIDE + y % SIDE) * CORES + core


def along(block, distance, phase):
    route = []
    for z, y, core in PLACES:
        if core == phase:
            target = node_of(z, y + distance, core)
        else:
            target = node_of(z + distance, y, core)
        route.append((node_of(z, y, core), target))
    return lax.ppermute(block, "node", route)


def other_core(block):
    route = [(node_of(z, y, core), node_of(z, y, 1 - core)) for z, y, core in PLACES]
    return lax.ppermute(block, "node", route)


def to_plane(block, pairs):
    return lax.ppermute(block, "layer", pairs)


def offered_rows(listed, rows):
    row_ids = lax.broadcasted_iota(jnp.int32, (rows.shape[0], listed.shape[1]), 0)
    selector = (row_ids == listed).astype(jnp.bfloat16)
    picked = lax.dot_general(
        selector, rows, (((0,), (0,)), ((), ())), preferred_element_type=jnp.float32
    )
    return picked.astype(jnp.bfloat16)


def first_kernel(place_ref, rows_ref, listed_ref, lists_ref, block_ref):
    span, node = place_ref[0], place_ref[1]
    offered = listed_ref.shape[2]
    nodes, picks = lists_ref.shape[2:]
    block_ref[pl.ds(offered, EXTRA), :] = jnp.zeros((EXTRA, block_ref.shape[1]), jnp.bfloat16)
    lists = lists_ref[span, 0].astype(jnp.float32).astype(jnp.bfloat16)
    for core in range(CORES):
        @pl.when(node % CORES == core)
        def _():
            for part in range(nodes // EXTRA):
                lanes = pl.ds(part * CORES * picks + core * picks, picks)
                block_ref[pl.ds(offered, EXTRA), lanes] = lists[part * EXTRA:(part + 1) * EXTRA]
    block_ref[pl.ds(0, offered), :] = offered_rows(listed_ref[span], rows_ref[...])


def selector_kernel(place_ref, listed_ref, selector_ref):
    listed = listed_ref[place_ref[0]]
    row_ids = lax.broadcasted_iota(jnp.int32, (selector_ref.shape[1], listed.shape[1]), 0)
    selector = (row_ids == listed).astype(jnp.float32)
    selector_ref[...] = jnp.transpose(selector).astype(jnp.bfloat16)


def layer_kernel(
    layer_id, first, last,
    place_ref, counts_ref, cols_ref, listed_ref, current_ref, previous_ref, tiles_ref, halves_ref, others_ref,
    *rest,
):
    mine_refs, theirs_refs, rest = rest[:SIDE], rest[SIDE:2 * SIDE], rest[2 * SIDE:]
    if not first:
        back_ref, *rest = rest
    outs = 1 if last else 3
    out_ref = rest[0]
    space, total = rest[outs:outs + 2]
    span, node = place_ref[0], place_ref[1]
    row_count = total.shape[0]
    offered = listed_ref.shape[0]
    z, y, core = node // (SIDE * CORES), (node // CORES) % SIDE, node % CORES
    each = mine_refs[0].shape[0] // SIDE
    if first:
        lists = rest[outs + 2]
        lane_block = pl.ds(pl.multiple_of((node // EXTRA) * TILE, TILE), TILE)
        wanted = lax.broadcasted_iota(jnp.int32, (EXTRA, TILE), 0) == node % EXTRA
    for refs, kind in ((mine_refs, core), (theirs_refs, 1 - core)):
        for j in range(SIDE):
            for k in range(SIDE):
                dz = jnp.where(kind == 0, j, k)
                dy = jnp.where(kind == 0, k, j)
                chip = ((z + SIDE - dz) % SIDE) * SIDE + (y + SIDE - dy) % SIDE
                start = pl.multiple_of(2 * row_count + (chip * CORES + kind) * offered, offered)
                space[pl.ds(start, offered), :] = refs[j][pl.ds(k * each, offered), :]
                if first:
                    raw = refs[j][pl.ds(k * each + offered, EXTRA), lane_block].astype(jnp.float32)
                    row = jnp.sum(jnp.where(wanted, raw, 0.0), axis=0, keepdims=True)
                    lists[pl.ds(chip + kind * SIDE * SIDE, 1), :] = row
    space[pl.ds(0, row_count), :] = current_ref[...]

    @pl.when(span == 0)
    def _():
        space[pl.ds(row_count, row_count), :] = jnp.zeros((row_count, space.shape[1]), space.dtype)

    @pl.when(span > 0)
    def _():
        space[pl.ds(row_count, row_count), :] = previous_ref[...]

    if first:
        wide_ref = rest[2]
        lanes = lax.broadcasted_iota(jnp.int32, (1, TILE), 1)
        shift = jnp.where(lanes >= TILE // CORES, offered, 0)
        slot_rows = lax.broadcasted_iota(jnp.int32, (CORES * offered, TILE), 0)

    ends = []
    reached = 0
    for r in range(counts_ref.shape[1] - 1):
        reached = reached + counts_ref[span, r]
        ends.append(reached)
    own_tiles = 2 * row_count // TILE
    begins = [0] + ends
    for f in range(cols_ref.shape[1]):
        owner = sum((f >= end).astype(jnp.int32) for end in ends)
        col = cols_ref[span, f]
        if first:
            plain = lanes + TILE * (col % CORES)
            chip = jnp.maximum(col - own_tiles, 0)
            listed = lists[pl.ds(chip, 1), :] + lists[pl.ds(chip + SIDE * SIDE, 1), :]
            listed = listed.astype(jnp.int32) + shift
            target = jnp.where(col < own_tiles, plain, listed)
            selector = (slot_rows == target).astype(jnp.bfloat16)
            wide = lax.dot_general(
                tiles_ref[f], selector, (((1,), (1,)), ((), ())), preferred_element_type=jnp.float32
            ).astype(jnp.bfloat16)
            wide_ref[f] = wide
        else:
            wide = tiles_ref[f]
        slot = jnp.where(col < own_tiles, col // CORES, col - own_tiles // CORES)
        row_at = pl.ds(pl.multiple_of(owner * TILE, TILE), TILE)
        slot_at = pl.ds(pl.multiple_of(slot * CORES * offered, CORES * offered), CORES * offered)
        product = jnp.dot(wide, space[slot_at, :], preferred_element_type=jnp.float32)
        opens = functools.reduce(jnp.logical_or, [f == begin for begin in begins])
        total[row_at, :] = jnp.where(opens, product, total[row_at, :] + product)
    half = halves_ref.shape[0] // SIDE
    distance = (span + SIDE - layer_id) % SIDE
    held = pl.ds(pl.multiple_of(distance * half, half), half)
    linear = 0.0
    for ref, kind in ((halves_ref, core), (others_ref, 1 - core)):
        columns = pl.ds(pl.multiple_of(kind * half, half), half)
        aggregate = total[:, columns].astype(jnp.bfloat16)
        linear = linear + jnp.dot(aggregate, ref[held, :], preferred_element_type=jnp.float32)
    fresh = jnp.maximum(linear, 0.0).astype(jnp.bfloat16)
    out_ref[...] = fresh
    if not last:
        picked = jnp.dot(listed_ref[...], fresh, preferred_element_type=jnp.float32)
        rest[1][...] = picked.astype(jnp.bfloat16)
    if not first and not last:
        moved_ref = rest[2]

        @pl.when(span == layer_id)
        def _():
            moved_ref[...] = back_ref[...]

        @pl.when(span != layer_id)
        def _():
            moved_ref[...] = fresh


def place_kernel(*refs):
    out_ref, sems = refs[-2:]
    spans = out_ref.shape[0]
    span = lax.axis_index("layer")
    first_ref = 0
    for layer_id in range(spans):
        parts = [0, 1, 2, 2, 3] if layer_id == spans - 1 else list(range(spans))
        sources = refs[first_ref:first_ref + len(parts)]
        first_ref += len(parts)

        @pl.when(span == layer_id)
        def _():
            copies, start = [], 0
            for i, (distance, source) in enumerate(zip(parts, sources)):
                rows = source.shape[0]
                target = out_ref.at[(layer_id - distance) % spans, pl.ds(start % out_ref.shape[1], rows)]
                start += rows
                piece = rows // PIECES
                for at in range(PIECES):
                    within = pl.ds(at * piece, piece)
                    sem = sems.at[i * PIECES + at]
                    copies.append(pltpu.make_async_copy(source.at[within], target.at[within], sem))
            for copy in copies:
                copy.start()
            for copy in copies:
                copy.wait()


def on_device(features, weights, boundary, pick_index, counts, tile_cols, tile_vals):
    spans, row_count, width = features.shape
    layers = lax.axis_size("layer")
    nodes = lax.axis_size("node")
    offered = boundary.shape[2]
    tile_total = tile_vals.shape[2]
    node = lax.axis_index("node")
    span = lax.axis_index("layer")
    place = jnp.stack([span, node]).astype(jnp.int32)
    current = lax.dynamic_index_in_dim(features, span, 0, keepdims=False)
    selector = pl.pallas_call(
        selector_kernel,
        out_shape=jax.ShapeDtypeStruct((offered, row_count), jnp.bfloat16),
        in_specs=[SMEM, VMEM],
        out_specs=VMEM,
        compiler_params=pltpu.CompilerParams(vmem_limit_bytes=16 << 20),
    )(place, boundary)
    counts, tile_cols = counts[:, 0], tile_cols[:, 0]
    rows_shape = jax.ShapeDtypeStruct((row_count, width), jnp.bfloat16)
    wide_shape = jax.ShapeDtypeStruct((tile_total, TILE, CORES * offered), jnp.bfloat16)
    block_shape = jax.ShapeDtypeStruct((offered, width), jnp.bfloat16)
    params = pltpu.CompilerParams(vmem_limit_bytes=16 << 20)
    block = pl.pallas_call(
        first_kernel,
        out_shape=jax.ShapeDtypeStruct((offered + EXTRA, width), jnp.bfloat16),
        in_specs=[SMEM, VMEM, VMEM, VMEM],
        out_specs=VMEM,
        compiler_params=params,
    )(place, current, boundary, pick_index)
    previous = lax.dynamic_index_in_dim(features, jnp.maximum(span - 1, 0), 0, keepdims=False)
    tiles = lax.dynamic_index_in_dim(tile_vals, span, 0, keepdims=False)[0]
    known = forward = back = None
    placed = []
    for layer_id in range(layers):
        first, last = layer_id == 0, layer_id == layers - 1
        row = jnp.concatenate([block] + [along(block, k, 0) for k in range(1, SIDE)], 0)
        if first:
            half = lax.dynamic_slice_in_dim(weights[0], (node % CORES) * (width // CORES), width // CORES, 0)
            halves = [half]
            for distance in range(1, layers):
                halves.append(to_plane(half, [(i, (i + distance) % layers) for i in range(layers)]))
            halves = jnp.concatenate(halves, 0)
            known = [halves, other_core(halves)]
        mine = [row] + [along(row, j, 1) for j in range(1, SIDE)]
        theirs = [other_core(part) for part in mine]
        if back is not None:
            previous = forward
            placed.append([current, forward, None, back])
        scratch = [
            pltpu.VMEM((2 * row_count + nodes * offered, width), jnp.bfloat16),
            pltpu.VMEM((row_count, width), jnp.float32),
        ]
        if first:
            scratch.append(pltpu.VMEM((CORES * SIDE * SIDE, TILE), jnp.float32))
        outs = [rows_shape] if last else [rows_shape, block_shape]
        if first:
            outs.append(wide_shape)
        elif not last:
            outs.append(rows_shape)
        results = pl.pallas_call(
            functools.partial(layer_kernel, layer_id, first, last),
            out_shape=outs,
            in_specs=[SMEM, SMEM, SMEM] + [VMEM] * (6 + 2 * SIDE + (not first)),
            out_specs=[VMEM] * len(outs),
            scratch_shapes=scratch,
            compiler_params=params,
        )(place, counts, tile_cols, selector, current, previous, tiles, *known, *mine, *theirs, *([] if first else [back]))
        current = results[0]
        if not last:
            block = results[1]
        if first:
            tiles = results[2]
        before, after, across = [(layer_id + step) % layers for step in (3, 1, 2)]
        if not last:
            forward = to_plane(current, [(i, (i + 1) % layers) for i in range(layers)])
            pairs = [(after, layer_id), (across, after)]
            moved = current
            if not first:
                pairs.append((layer_id, before))
                moved = results[2]
            back = to_plane(moved, pairs)
            if not first:
                placed[-1][2] = back
        else:
            half = row_count // 2
            relayed = to_plane(current[:half], [(across, before)])
            placed[-1][2] = to_plane(back, [(layer_id, before)])
            placed.append([
                current,
                to_plane(current, [(before, layer_id)]),
                to_plane(relayed, [(before, layer_id)]),
                to_plane(current[half:], [(across, layer_id)]),
                to_plane(current, [(after, layer_id)]),
            ])
    placed = sum(placed, [])
    return pl.pallas_call(
        place_kernel,
        out_shape=jax.ShapeDtypeStruct(features.shape, features.dtype),
        in_specs=[VMEM] * len(placed),
        out_specs=HBM,
        scratch_shapes=[pltpu.SemaphoreType.DMA((5 * PIECES,))],
        compiler_params=params,
    )(*placed)


def solution(mesh):
    return jax.shard_map(
        on_device,
        mesh=mesh,
        in_specs=(
            P(None, "node", None),
            P("layer", None, None),
            P(None, "node", None),
            P(None, "node", None, None),
            P(None, "node", None),
            P(None, "node", None),
            P(None, "node", None, None, None),
        ),
        out_specs=P(None, "node", "layer"),
        check_vma=False,
    )
```
